32 devices in a mesh: gy: 4 (over y, core), gz: 8 (over z, x).
Axes of the slice: x: 2, y: 2, z: 4, core: 2. Of those that a mesh axis runs over, the one named last changes fastest.
Arguments:
- linear_field: bfloat16 [3, 16, 64, 128], P(None, 'gy', 'gz'), may hold values from -6 to 6
- lift_kernel: bfloat16 [27, 32, 3], replicated, may hold values from -1 to 1
- fine_kernel: bfloat16 [27, 32, 32], replicated, may hold values from -0.3125 to 0.3125
- reduce_first: bfloat16 [8, 64, 32], replicated, may hold values from -0.5 to 0.5
- middle_kernel: bfloat16 [27, 64, 64], replicated, may hold values from -0.21875 to 0.21875
- reduce_second: bfloat16 [8, 128, 64], replicated, may hold values from -0.375 to 0.375
- coarse_kernel: bfloat16 [27, 128, 128], replicated, may hold values from -0.15625 to 0.15625
- expand_second: bfloat16 [8, 64, 128], replicated, may hold values from -0.75 to 0.75
- merge_middle: bfloat16 [27, 64, 128], replicated, may hold values from -0.15625 to 0.15625
- expand_first: bfloat16 [8, 32, 64], replicated, may hold values from -1 to 1
- merge_fine: bfloat16 [27, 32, 64], replicated, may hold values from -0.21875 to 0.21875
- output_head: bfloat16 [3, 32], replicated, may hold values from -1 to 1
Outputs:
- displacement: float32 [3, 16, 64, 128], P(None, 'gy', 'gz')
The draws below stay inside these ranges and needn't reach their ends.
All inputs are finite; a program needn't handle non-finite values.
Results may differ from the reference program's by a relative error of at most 0.015.
Values may be sent and summed in bfloat16 or wider, within the bound.
No kernel may reach another device: no remote copies, remote signals or barrier semaphores. Data moves between devices by JAX's collectives and lax.ppermute only.
A program may use at most 64 MiB of HBM per device.

```python
import jax
import jax.numpy as jnp
from jax import lax

C0 = 32
C1 = 64
C2 = 128
NX = 128
NY = 16
NZ = 64


def block_levels(stream_key, dims, cuts, smallest, high):
    factor_of = 1.0
    for axis_at, shards_of in cuts:
        heights = jax.random.uniform(jax.random.fold_in(jax.random.fold_in(stream_key, 6), axis_at), (shards_of,), jnp.float32, smallest / len(cuts), high / len(cuts))
        factor_of = factor_of * jnp.repeat(jnp.exp(heights), dims[axis_at] // shards_of).reshape((-1,) + (1,) * (len(dims) - 1 - axis_at))
    return factor_of


def noise(stream_key, extent, scale, reach, split=(), kind=jnp.bfloat16):
    level = block_levels(stream_key, extent, split, -0.22, 0.18) if split else 1.0
    entries = jax.random.normal(stream_key, extent, jnp.float32) * scale * level
    return jnp.minimum(jnp.maximum(entries, -reach), reach).astype(kind)


def setup_inputs(seed: int = 0) -> dict:
    key_of = jax.random.split(jax.random.key(seed), 13)
    return {
        "linear_field": noise(key_of[0], (3, NY, NZ, NX), 1.0, 6.0, ((1, 4), (2, 8))),
        "lift_kernel": noise(key_of[1], (27, C0, 3), (81 // 2) ** -0.5, 1.0),
        "fine_kernel": noise(key_of[2], (27, C0, C0), (27 * C0 // 2) ** -0.5, 0.3125),
        "reduce_first": noise(key_of[3], (8, C1, C0), (4 * C0) ** -0.5, 0.5),
        "middle_kernel": noise(key_of[4], (27, C1, C1), (27 * C1 // 2) ** -0.5, 0.21875),
        "reduce_second": noise(key_of[5], (8, C2, C1), (4 * C1) ** -0.5, 0.375),
        "coarse_kernel": noise(key_of[6], (27, C2, C2), (27 * C2 // 2) ** -0.5, 0.15625),
        "expand_second": noise(key_of[7], (8, C1, C2), (C2 // 2) ** -0.5, 0.75),
        "merge_middle": noise(key_of[8], (27, C1, 2 * C1), (27 * C1) ** -0.5, 0.15625),
        "expand_first": noise(key_of[9], (8, C0, C1), (C1 // 2) ** -0.5, 1.0),
        "merge_fine": noise(key_of[10], (27, C0, 2 * C0), (27 * C0) ** -0.5, 0.21875),
        "output_head": noise(key_of[11], (3, C0), C0 ** -0.5, 1.0),
    }


def activate(values):
    return jax.nn.leaky_relu(values, 0.1).astype(jnp.bfloat16)


def convolve(field, kernel):
    outs_c = kernel.shape[1]
    ins_c = kernel.shape[2]
    padded = jnp.pad(field.astype(jnp.float32), ((0, 0), (1, 1), (1, 1), (1, 1)), mode="wrap")
    filters = kernel.astype(jnp.float32).reshape(3, 3, 3, outs_c, ins_c).transpose(3, 4, 0, 1, 2)
    result = lax.conv_general_dilated(padded[None], filters, (1, 1, 1), "VALID", dimension_numbers=("NCDHW", "OIDHW", "NCDHW"), precision=lax.Precision.HIGHEST)
    return result[0]


def coarsen(field, kernel):
    chans, size_y, size_z, size_x = field.shape
    blocks = field.astype(jnp.float32).reshape(chans, size_y // 2, 2, size_z // 2, 2, size_x // 2, 2)
    taps = kernel.astype(jnp.float32).reshape(2, 2, 2, kernel.shape[1], kernel.shape[2])
    return jnp.einsum("abcoi,iyazbxc->oyzx", taps, blocks, precision=lax.Precision.HIGHEST)


def refine(field, kernel):
    chans, size_y, size_z, size_x = field.shape
    taps = kernel.astype(jnp.float32).reshape(2, 2, 2, kernel.shape[1], kernel.shape[2])
    spread = jnp.einsum("abcoi,iyzx->oyazbxc", taps, field.astype(jnp.float32), precision=lax.Precision.HIGHEST)
    return spread.reshape(kernel.shape[1], 2 * size_y, 2 * size_z, 2 * size_x)


def reference(linear_field, lift_kernel, fine_kernel, reduce_first, middle_kernel, reduce_second, coarse_kernel, expand_second, merge_middle, expand_first, merge_fine, output_head):
    lifted = activate(convolve(linear_field, lift_kernel))
    fine_skip = activate(convolve(lifted, fine_kernel))
    middle_in = activate(coarsen(fine_skip, reduce_first))
    middle_skip = activate(convolve(middle_in, middle_kernel))
    coarse_in = activate(coarsen(middle_skip, reduce_second))
    coarse_out = activate(convolve(coarse_in, coarse_kernel))
    joined = jnp.concatenate([activate(refine(coarse_out, expand_second)), middle_skip], axis=0)
    middle_out = activate(convolve(joined, merge_middle))
    fine_joined = jnp.concatenate([activate(refine(middle_out, expand_first)), fine_skip], axis=0)
    fine_out = activate(convolve(fine_joined, merge_fine))
    return jnp.einsum("oc,cyzx->oyzx", output_head.astype(jnp.float32), fine_out.astype(jnp.float32), precision=lax.Precision.HIGHEST)
```

```python
import functools

import jax
import jax.numpy as jnp
import numpy as np
from jax import lax
from jax.experimental import pallas as pl
from jax.experimental.pallas import tpu as pltpu
from jax.sharding import PartitionSpec as P

BF = jnp.bfloat16
F32 = jnp.float32
VMEM = pl.BlockSpec(memory_space=pltpu.VMEM)
SMEM = pl.BlockSpec(memory_space=pltpu.SMEM)


def act(values):
    return jnp.maximum(values, 0.1 * values)


def dot(left, right):
    return jnp.dot(left, right, preferred_element_type=F32)


def split_fine():
    m = np.zeros((256, 256), np.float32)
    for row in range(2):
        for x in range(128):
            m[row * 128 + x, (x % 2) * 128 + row * 64 + x // 2] = 1
    return m


def split_middle():
    m = np.zeros((512, 512), np.float32)
    for row in range(4):
        for b in range(2):
            for x in range(64):
                m[row * 128 + b * 64 + x, (2 * b + x % 2) * 128 + row * 32 + x // 2] = 1
    return m


def coarse_taps():
    m = np.zeros((256, 9 * 128), np.float32)
    for dz in range(3):
        for dx in range(3):
            for row in range(4):
                for x in range(32):
                    m[(row + dz) * 32 + (x + dx - 1) % 32, (3 * dz + dx) * 128 + row * 32 + x] = 1
    return m


def lift_spread():
    m = np.zeros((81, 512), np.float32)
    for dy in range(3):
        for dz in range(3):
            for dx in range(3):
                for c in range(3):
                    m[(9 * dy + 3 * dz + dx) * 3 + c, ((dy * 3 + c) * 3 + dx) * 16 + dz] = 1
    return m


def prep_kernel(lift, fine, red1, mid, red2, mfine, spread, t_o, wf_o, wd1_o, wm_o, wd2_o, wmf_o):
    base = dot(lift[...], spread[...])
    for zo in range(8):
        moved = base if zo == 0 else pltpu.roll(base, zo, 1)
        t_o[32 * zo : 32 * zo + 32] = moved[:, :432].astype(BF)
    for dz in range(3):
        for dy in range(3):
            for dx in range(3):
                k = 3 * dy + dx
                wf_o[32 * dz : 32 * dz + 32, 32 * k : 32 * k + 32] = fine[9 * dy + 3 * dz + dx]
                wmf_o[32 * dz : 32 * dz + 32, 64 * k : 64 * k + 64] = mfine[9 * dy + 3 * dz + dx]
                j = 3 * dz + dx
                wm_o[64 * dy : 64 * dy + 64, 64 * j : 64 * j + 64] = mid[9 * dy + 3 * dz + dx]
    for t in range(8):
        wd1_o[:, 32 * t : 32 * t + 32] = red1[t]
        wd2_o[:, 64 * t : 64 * t + 64] = red2[t]


class Rows:
    def __init__(self, low, count, periodic):
        self.low, self.count, self.periodic = low, count, periodic

    def at(self, rel):
        if self.periodic:
            moved = rel - self.low + 4 * self.count
            return moved % self.count if isinstance(moved, int) else lax.rem(moved, self.count)
        return rel - self.low


def levels(periodic):
    if periodic:
        fine, mid, coarse = Rows(-8, 16, True), Rows(-4, 8, True), Rows(-2, 4, True)
        return fine, fine, fine, mid, mid, coarse
    return (
        Rows(-12, 28, False),
        Rows(-11, 26, False),
        Rows(-10, 24, False),
        Rows(-5, 12, False),
        Rows(-4, 10, False),
        Rows(-2, 5, False),
    )


def shifted_64(v, lane):
    edge_low = (lane % 64) == 0
    edge_high = (lane % 64) == 63
    low = jnp.where(edge_low, pltpu.roll(v, 65, 1), pltpu.roll(v, 1, 1))
    high = jnp.where(edge_high, pltpu.roll(v, 63, 1), pltpu.roll(v, 127, 1))
    return low, high


def net_kernel(
    periodic,
    me,
    lin,
    t_w,
    wf,
    wd1,
    wm,
    wd2,
    ck,
    we2,
    mmk,
    we1,
    wmf,
    head,
    s_fine,
    s_fine_t,
    s_mid,
    s_mid_t,
    s_taps,
    out,
    pat,
    lifted,
    fine,
    halves,
    mids,
    mskip,
    quarters,
    ctaps,
    ups,
    joined,
    mout,
    jfine,
):
    r_lin, r_lift, r_fine, r_mid, r_skip, r_coarse = levels(periodic)
    blocks = lin.shape[0]

    def patch(k, carry):
        block = lax.rem(me[0] + k // 4 + (blocks - 2), blocks) if periodic else k // 4
        for c in range(3):
            mid_v = lin[block, c, lax.rem(k, 4)].astype(F32)
            for dx, v in enumerate((pltpu.roll(mid_v, 1, 1), mid_v, pltpu.roll(mid_v, 127, 1))):
                v = jnp.concatenate([v, jnp.zeros((8, 128), F32)], axis=0)
                for j in range(4):
                    pat[k, j, (3 * c + dx) * 16 : (3 * c + dx) * 16 + 16] = v[8 * j : 8 * j + 16].astype(BF)
        return carry

    lax.fori_loop(0, r_lin.count, patch, 0)

    def lift(k, carry):
        rel = k + r_lift.low
        ys = [r_lin.at(rel + dy) for dy in (-1, 0, 1)]
        for pair in range(2):
            cols = [jnp.concatenate([pat[y, 2 * pair + h] for y in ys], axis=0) for h in range(2)]
            r = act(dot(t_w[...], jnp.concatenate(cols, axis=1)))
            for h in range(2):
                for zo in range(8):
                    z = 16 * pair + 8 * h + zo
                    if z < 30:
                        v = r[32 * zo : 32 * zo + 32, 128 * h : 128 * h + 128]
                        lifted[k, z, 0:32] = pltpu.roll(v, 1, 1).astype(BF)
                        lifted[k, z, 32:64] = v.astype(BF)
                        lifted[k, z, 64:96] = pltpu.roll(v, 127, 1).astype(BF)
        return carry

    lax.fori_loop(0, r_lift.count, lift, 0)

    def fine_conv(k, carry):
        rel = k + r_fine.low
        ys = [r_lift.at(rel + dy) for dy in (-1, 0, 1)]
        parts = []
        for pair in range(15):
            cols = [jnp.concatenate([lifted[y, 2 * pair + h] for y in ys], axis=0) for h in range(2)]
            r = dot(wf[...], jnp.concatenate(cols, axis=1))
            parts += [r[:, :128], r[:, 128:]]
        rows = []
        for z in range(28):
            v = parts[z][0:32] + parts[z + 1][32:64] + parts[z + 2][64:96]
            v = act(v).astype(BF)
            fine[k, z] = v
            rows.append(v)
        left = []
        for p in range(7):
            for b in range(2):
                left.append(jnp.concatenate([rows[4 * p + b], rows[4 * p + 2 + b]], axis=1))
        s = dot(jnp.concatenate(left, axis=0), s_fine[...]).astype(BF)
        for i in range(14):
            for c in range(2):
                halves[k, i // 2, (2 * (i % 2) + c) * 32 : (2 * (i % 2) + c) * 32 + 32] = s[
                    32 * i : 32 * i + 32, 128 * c : 128 * c + 128
                ]
        return carry

    lax.fori_loop(0, r_fine.count, fine_conv, 0)

    lane = lax.broadcasted_iota(jnp.int32, (64, 128), 1)

    def middle_in(k, carry):
        direct = [[], []]
        for p in range(7):
            cols = []
            for h in range(2):
                rel = 2 * (2 * k + h + r_mid.low)
                cols.append(jnp.concatenate([halves[r_fine.at(rel + a), p] for a in range(2)], axis=0))
            r = act(dot(wd1[...], jnp.concatenate(cols, axis=1)))
            for h in range(2):
                direct[h].append(r[:, 128 * h : 128 * h + 128])
        for h in range(2):
            turned = [pltpu.roll(v, 64, 1) for v in direct[h]]
            for pos in range(13):
                p = pos // 2
                v = direct[h][p] if pos % 2 == 0 else jnp.where(lane < 64, turned[p], turned[p + 1])
                low, high = shifted_64(v, lane)
                for dx, u in enumerate((low, v, high)):
                    at = pos * 192 + dx * 64
                    mids[2 * k + h, at : at + 64] = u.astype(BF)
        return carry

    lax.fori_loop(0, r_mid.count // 2, middle_in, 0)

    def middle_conv(k, carry):
        parts = []
        start = pl.multiple_of(k * 384, 384)
        for pair in range(r_mid.count // 2):
            cols = [mids[2 * pair + h, pl.ds(start, 576)] for h in range(2)]
            r = dot(wm[...], jnp.concatenate(cols, axis=1))
            parts += [r[:, :128], r[:, 128:]]
        for y in range(r_skip.count):
            rel = y + r_skip.low
            v = sum(parts[r_mid.at(rel + dy - 1)][64 * dy : 64 * dy + 64] for dy in range(3))
            mskip[y, k] = act(v).astype(BF)
        return carry

    lax.fori_loop(0, 6, middle_conv, 0)

    for chunk in range(2):
        width = 4 if chunk == 0 else 2
        left = [
            jnp.concatenate([mskip[y, 4 * chunk + q] for q in range(width)], axis=1) for y in range(r_skip.count)
        ]
        s = dot(jnp.concatenate(left, axis=0), s_mid[: 128 * width]).astype(BF)
        for y in range(r_skip.count):
            for t in range(4):
                quarters[y, t * 64 : t * 64 + 64, 128 * chunk : 128 * chunk + 128] = s[
                    64 * y : 64 * y + 64, 128 * t : 128 * t + 128
                ]
    for y in range(r_coarse.count):
        rel = 2 * (y + r_coarse.low)
        right = jnp.concatenate([quarters[r_skip.at(rel + a)] for a in range(2)], axis=0)
        cin = act(dot(wd2[...], right)).astype(BF)
        taps = dot(cin, s_taps[...]).astype(BF)
        for t in range(9):
            ctaps[y, 128 * t : 128 * t + 128] = taps[:, 128 * t : 128 * t + 128]

    wc = jnp.concatenate([ck[t] for t in range(27)], axis=1)
    for first in (-1, 1):
        rels = (first, first + 1) if first < 1 else (first, first)
        cols = [jnp.concatenate([ctaps[r_coarse.at(rel + dy)] for dy in (-1, 0, 1)], axis=0) for rel in rels]
        cout = act(dot(wc, jnp.concatenate(cols, axis=1))).astype(BF)
        u = act(dot(we2[...], cout)).astype(BF)
        for h in range(2 if first < 1 else 1):
            for a in range(2):
                left = jnp.concatenate(
                    [u[(4 * a + t) * 64 : (4 * a + t) * 64 + 64, 128 * h : 128 * h + 128] for t in range(4)], axis=1
                )
                s = dot(left, s_mid_t[...]).astype(BF)
                for q in range(4):
                    ups[2 * (first + 1 + h) + a, q] = s[:, 128 * q : 128 * q + 128]

    lane128 = lax.broadcasted_iota(jnp.int32, (128, 128), 1)
    for y in range(6):
        direct = [
            jnp.concatenate([ups[y, q], mskip[r_skip.at(y - 2), q + 1]], axis=0).astype(F32) for q in range(4)
        ]
        turned = [pltpu.roll(v, 64, 1) for v in direct]
        for pos in range(7):
            p = pos // 2
            v = direct[p] if pos % 2 == 0 else jnp.where(lane128 < 64, turned[p], turned[p + 1])
            low, high = shifted_64(v, lane128)
            for dx, u in enumerate((low, v, high)):
                at = pos * 384 + dx * 128
                joined[y, at : at + 128] = u.astype(BF)
    wmm = jnp.concatenate(
        [
            jnp.concatenate([mmk[9 * dy + 3 * dz + dx] for dz in range(3) for dx in range(3)], axis=1)
            for dy in range(3)
        ],
        axis=0,
    )
    for k in range(3):
        parts = []
        for pair in range(3):
            cols = [joined[2 * pair + h, 768 * k : 768 * k + 1152] for h in range(2)]
            r = dot(wmm, jnp.concatenate(cols, axis=1))
            parts += [r[:, :128], r[:, 128:]]
        for y in range(4):
            v = parts[y][0:64] + parts[y + 1][64:128] + parts[y + 2][128:192]
            mout[y, k] = act(v).astype(BF)

    for y in range(4):
        for k in range(3):
            u = act(dot(we1[...], mout[y, k])).astype(BF)
            left = []
            for ab in range(4):
                left.append(jnp.concatenate([u[64 * ab : 64 * ab + 32], u[64 * ab + 32 : 64 * ab + 64]], axis=1))
            s = dot(jnp.concatenate(left, axis=0), s_fine_t[...])
            for a in range(2):
                yf = 2 * (y - 1) + a
                if not -1 <= yf <= 4:
                    continue
                for b in range(2):
                    for h in range(2):
                        zf = -2 + 4 * k + 2 * h + b
                        if not -1 <= zf <= 8:
                            continue
                        up = s[(2 * a + b) * 32 : (2 * a + b) * 32 + 32, 128 * h : 128 * h + 128]
                        skip = fine[r_fine.at(yf), zf + 10].astype(F32)
                        v = jnp.concatenate([up, skip], axis=0)
                        jfine[yf + 1, zf + 1, 0:64] = pltpu.roll(v, 1, 1).astype(BF)
                        jfine[yf + 1, zf + 1, 64:128] = v.astype(BF)
                        jfine[yf + 1, zf + 1, 128:192] = pltpu.roll(v, 127, 1).astype(BF)

    for y in range(4):
        parts = []
        for pair in range(5):
            cols = [jnp.concatenate([jfine[y + dy, 2 * pair + h] for dy in range(3)], axis=0) for h in range(2)]
            r = dot(wmf[...], jnp.concatenate(cols, axis=1))
            parts += [r[:, :128], r[:, 128:]]
        rows = []
        for z in range(8):
            v = parts[z][0:32] + parts[z + 1][32:64] + parts[z + 2][64:96]
            rows.append(act(v).astype(BF))
        d = dot(head[...], jnp.concatenate(rows, axis=1))
        for z in range(8):
            for o in range(3):
                out[o, y, z : z + 1, :] = d[o : o + 1, 128 * z : 128 * z + 128]


def ring(axis, hops):
    count = lax.axis_size(axis)
    return [(i, (i + hops) % count) for i in range(count)]


def body(
    linear_field,
    lift_kernel,
    fine_kernel,
    reduce_first,
    middle_kernel,
    reduce_second,
    coarse_kernel,
    expand_second,
    merge_middle,
    expand_first,
    merge_fine,
    output_head,
):
    send = functools.partial(lax.ppermute, axis_name="gz")
    below = send(linear_field, perm=ring("gz", 1))
    above = send(linear_field, perm=ring("gz", -1))
    below_2 = send(linear_field[:, :, 4:], perm=ring("gz", 2))
    above_2 = send(linear_field[:, :, :4], perm=ring("gz", -2))
    wide = jnp.concatenate([below_2, below, linear_field, above, above_2], axis=2)
    count_y = lax.axis_size("gy")
    periodic = count_y == 4
    if periodic:
        lin = lax.all_gather(wide, "gy")
    else:
        lin = jnp.stack([wide if h == 0 else lax.ppermute(wide, "gy", ring("gy", -h)) for h in range(-3, 4)])
    me = lax.axis_index("gy").astype(jnp.int32).reshape(1)

    lift_flat = lift_kernel.transpose(1, 0, 2).reshape(32, 81)
    t_w, wf, wd1, wm, wd2, wmf = pl.pallas_call(
        prep_kernel,
        out_shape=[
            jax.ShapeDtypeStruct(s, BF)
            for s in ((256, 432), (96, 288), (64, 256), (192, 576), (128, 512), (96, 576))
        ],
        in_specs=[VMEM] * 7,
        out_specs=[VMEM] * 6,
        compiler_params=pltpu.CompilerParams(vmem_limit_bytes=16 << 20),
    )(lift_flat, fine_kernel, reduce_first, middle_kernel, reduce_second, merge_fine, lift_spread().astype(BF))

    r_lin, r_lift, r_fine, r_mid, r_skip, r_coarse = levels(periodic)
    split_f, split_m = split_fine().astype(BF), split_middle().astype(BF)
    head = jnp.pad(output_head, ((0, 13), (0, 0)))
    scratch = [
        pltpu.VMEM((r_lin.count, 4, 144, 128), BF),
        pltpu.VMEM((r_lift.count, 30, 96, 128), BF),
        pltpu.VMEM((r_fine.count, 28, 32, 128), BF),
        pltpu.VMEM((r_fine.count, 7, 128, 128), BF),
        pltpu.VMEM((r_mid.count, 13 * 192, 128), BF),
        pltpu.VMEM((r_skip.count, 6, 64, 128), BF),
        pltpu.VMEM((r_skip.count, 256, 256), BF),
        pltpu.VMEM((r_coarse.count, 1152, 128), BF),
        pltpu.VMEM((6, 4, 64, 128), BF),
        pltpu.VMEM((6, 7 * 384, 128), BF),
        pltpu.VMEM((4, 3, 64, 128), BF),
        pltpu.VMEM((6, 10, 192, 128), BF),
    ]
    return pl.pallas_call(
        functools.partial(net_kernel, periodic),
        out_shape=jax.ShapeDtypeStruct(linear_field.shape, F32),
        in_specs=[SMEM] + [VMEM] * 17,
        out_specs=VMEM,
        scratch_shapes=scratch,
        compiler_params=pltpu.CompilerParams(vmem_limit_bytes=56 << 20),
    )(
        me,
        lin,
        t_w,
        wf,
        wd1,
        wm,
        wd2,
        coarse_kernel,
        expand_second.reshape(512, 128),
        merge_middle,
        expand_first.reshape(256, 64),
        wmf,
        head,
        split_f,
        np.ascontiguousarray(split_f.T),
        split_m,
        np.ascontiguousarray(split_m.T),
        coarse_taps().astype(BF),
    )


def solution(mesh):
    return jax.shard_map(
        body,
        mesh=mesh,
        in_specs=(P(None, "gy", "gz", None), P(), P(), P(), P(), P(), P(), P(), P(), P(), P(), P()),
        out_specs=P(None, "gy", "gz", None),
        check_vma=False,
    )
```

```python
import functools

import jax
import jax.numpy as jnp
from jax import lax
from jax.experimental import pallas as pl
from jax.experimental.pallas import tpu as pltpu
from jax.sharding import PartitionSpec as P

BF = jnp.bfloat16
F32 = jnp.float32
VMEM = pl.BlockSpec(memory_space=pltpu.VMEM)
ANY = pl.BlockSpec(memory_space=pl.ANY)
HBM = pl.BlockSpec(memory_space=pltpu.HBM)
SMEM = pl.BlockSpec(memory_space=pltpu.SMEM)


def act(values):
    return jnp.maximum(values, 0.1 * values)


def dot(left, right):
    return jnp.dot(left, right, preferred_element_type=F32)


def iotas(rows, columns):
    return (
        lax.broadcasted_iota(jnp.int32, (rows, columns), 0),
        lax.broadcasted_iota(jnp.int32, (rows, columns), 1),
    )


def chosen(test):
    return jnp.where(test, 1.0, 0.0).astype(BF)


def fine_order(i):
    return ((i & 1) << 7) | ((i >> 7) << 6) | ((i & 127) >> 1)


def middle_order(i):
    return (((i >> 6) & 1) << 8) | ((i & 1) << 7) | ((i >> 7) << 5) | ((i & 63) >> 1)


def coarse_tap(dz, dx):
    r, c = iotas(256, 128)
    return chosen(r == ((((c >> 5) + dz) << 5) | ((c + dx - 1) & 31)))


def lift_spread(c):
    r, col = iotas(27, 512)
    return chosen(col == ((r // 9 * 3 + c) * 3 + r % 3) * 16 + r // 3 % 3)


def prep_kernel(lift, *refs):
    sources, refs = refs[:5], refs[5:]
    results, refs = refs[:12], refs[12:]
    (t_o, wf_o, wf9_o, wd1_o, wm_o, wd2_o, wmf_o, sf_o, sft_o, sm_o, smt_o, st_o), refs = refs[:12], refs[12:]
    (fine, red1, mid, red2, mfine), sems, out_sems = refs[:5], refs[5], refs[6]
    copies = [pltpu.make_async_copy(src, dst, sems.at[i]) for i, (src, dst) in enumerate(zip(sources, refs))]
    for copy in copies:
        copy.start()
    r, c = iotas(256, 256)
    sf_o[...] = chosen(fine_order(r) == c)
    sft_o[...] = chosen(r == fine_order(c))
    r, c = iotas(512, 512)
    sm_o[...] = chosen(middle_order(r) == c)
    smt_o[...] = chosen(r == middle_order(c))
    for t in range(9):
        st_o[:, 128 * t : 128 * t + 128] = coarse_tap(t // 3, t % 3)
    base = sum(
        lax.dot_general(lift[c], lift_spread(c), (((0,), (0,)), ((), ())), preferred_element_type=F32)
        for c in range(3)
    )
    for zo in range(8):
        moved = base if zo == 0 else pltpu.roll(base, zo, 1)
        t_o[32 * zo : 32 * zo + 32] = moved[:, :432].astype(BF)
    for copy in copies:
        copy.wait()
    for dz in range(3):
        for dy in range(3):
            for dx in range(3):
                k = 3 * dy + dx
                if k < 8:
                    wf_o[32 * dz : 32 * dz + 32, 32 * k : 32 * k + 32] = fine[9 * dy + 3 * dz + dx]
                else:
                    wf9_o[:, 32 * dz : 32 * dz + 32] = fine[9 * dy + 3 * dz + dx]
                wmf_o[32 * dz : 32 * dz + 32, 64 * k : 64 * k + 64] = mfine[9 * dy + 3 * dz + dx]
                j = 3 * dz + dx
                wm_o[64 * dy : 64 * dy + 64, 64 * j : 64 * j + 64] = mid[9 * dy + 3 * dz + dx]
    wd1_o[...] = red1[...].astype(F32).T.astype(BF)
    wd2_o[...] = red2[...].astype(F32).T.astype(BF)
    made = (t_o, wf_o, wf9_o, wd1_o, wm_o, wd2_o, wmf_o, sf_o, sft_o, sm_o, smt_o, st_o)
    copies = [pltpu.make_async_copy(src, dst, out_sems.at[i]) for i, (src, dst) in enumerate(zip(made, results))]
    for copy in copies:
        copy.start()
    for copy in copies:
        copy.wait()


class Rows:
    def __init__(self, low, count, periodic):
        self.low, self.count, self.periodic = low, count, periodic

    def at(self, rel):
        if self.periodic:
            moved = rel - self.low + 4 * self.count
            return moved % self.count if isinstance(moved, int) else lax.rem(moved, self.count)
        return rel - self.low


def levels(periodic):
    if periodic:
        fine, mid, coarse = Rows(-8, 16, True), Rows(-4, 8, True), Rows(-2, 4, True)
        return fine, fine, fine, mid, mid, coarse
    return (
        Rows(-12, 28, False),
        Rows(-11, 26, False),
        Rows(-10, 24, False),
        Rows(-5, 12, False),
        Rows(-4, 10, False),
        Rows(-2, 5, False),
    )


def shifted_64(v, lane):
    edge_low = (lane & 63) == 0
    edge_high = (lane & 63) == 63
    low = jnp.where(edge_low, pltpu.roll(v, 65, 1), pltpu.roll(v, 1, 1))
    high = jnp.where(edge_high, pltpu.roll(v, 63, 1), pltpu.roll(v, 127, 1))
    return low, high


def net_kernel(periodic, me, *refs):
    count = 5 if periodic else 1
    fields, refs = refs[:count], refs[count:]
    head, weights, out, refs = refs[0], refs[1:17], refs[17], refs[18:]
    pat, lifted, fine, halves, mskip, quarters, ctaps, ups, mout, joined = refs[:10]
    held, sems = refs[10:26], refs[26]
    near_by, field_sems = refs[27 : 27 + count], refs[27 + count]
    field_copies = [
        pltpu.make_async_copy(src, dst, field_sems.at[i]) for i, (src, dst) in enumerate(zip(fields, near_by))
    ]
    for copy in field_copies:
        copy.start()
    if periodic:
        own, near, far, other_near, other_far = near_by
    else:
        wide = near_by[0]
    copies = [pltpu.make_async_copy(src, dst, sems.at[i]) for i, (src, dst) in enumerate(zip(weights, held))]
    for copy in copies:
        copy.start()
    (t_w, wf, wf9, wd1, wm, wd2, ck, we2, mmk, we1, wmf, s_fine, s_fine_t, s_mid, s_mid_t, s_taps) = held

    def need(*names):
        for name in names:
            copies[[h is name for h in held].index(True)].wait()

    r_lin, r_lift, r_fine, r_mid, r_skip, r_coarse = levels(periodic)
    core = lax.rem(me[0], 2)

    for copy in field_copies:
        copy.wait()

    def patch(k, carry):
        row = lax.rem(k, 4)
        if periodic:
            block = lax.rem(me[0] + k // 4 + 2, 4)
        for c in range(3):
            if periodic:
                mine = [ref[block, c, row].astype(F32) for ref in (near, far)]
                others = [ref[block, c, row].astype(F32) for ref in (other_near, other_far)]
                below_1, below_2 = (jnp.where(core == 0, m, t) for m, t in zip(mine, others))
                above_1, above_2 = (jnp.where(core == 0, t, m) for m, t in zip(mine, others))
                parts = [below_2[4:], below_1, own[block, c, row].astype(F32), above_1, above_2[:4]]
                mid_v = jnp.concatenate(parts, axis=0)
            else:
                mid_v = wide[k // 4, c, row].astype(F32)
            for dx, v in enumerate((pltpu.roll(mid_v, 1, 1), mid_v, pltpu.roll(mid_v, 127, 1))):
                v = jnp.concatenate([v, jnp.zeros((8, 128), F32)], axis=0)
                for j in range(4):
                    pat[k, j, (3 * c + dx) * 16 : (3 * c + dx) * 16 + 16] = v[8 * j : 8 * j + 16].astype(BF)
        return carry

    lax.fori_loop(0, r_lin.count, patch, 0)

    need(t_w)

    def lift(k, carry):
        rel = k + r_lift.low
        ys = [r_lin.at(rel + dy) for dy in (-1, 0, 1)]
        for pair in range(2):
            cols = [jnp.concatenate([pat[y, 2 * pair + h] for y in ys], axis=0) for h in range(2)]
            r = act(dot(t_w[...], jnp.concatenate(cols, axis=1)))
            for h in range(2):
                for zo in range(8):
                    z = 16 * pair + 8 * h + zo
                    if z < 30:
                        v = r[32 * zo : 32 * zo + 32, 128 * h : 128 * h + 128]
                        lifted[k, 96 * z : 96 * z + 32] = pltpu.roll(v, 1, 1).astype(BF)
                        lifted[k, 96 * z + 32 : 96 * z + 64] = v.astype(BF)
                        lifted[k, 96 * z + 64 : 96 * z + 96] = pltpu.roll(v, 127, 1).astype(BF)
        return carry

    lax.fori_loop(0, r_lift.count, lift, 0, unroll=2)

    need(wf, wf9, s_fine)

    def fine_conv(k, carry):
        rel = k + r_fine.low
        ys = [r_lift.at(rel + dy) for dy in (-1, 0, 1)]
        parts = []
        for pair in range(15):
            cols = [
                jnp.concatenate([*(lifted[y, 96 * (2 * pair + h) : 96 * (2 * pair + h) + 96] for y in ys[:2]), lifted[ys[2], 96 * (2 * pair + h) : 96 * (2 * pair + h) + 64]], axis=0)
                for h in range(2)
            ]
            r = dot(wf[...], jnp.concatenate(cols, axis=1))
            parts += [r[:, :128], r[:, 128:]]
        rows = []
        for pair in range(14):
            last = [lifted[ys[2], 96 * (2 * pair + i) + 64 : 96 * (2 * pair + i) + 96] for i in range(4)]
            cols = [jnp.concatenate(last[h : h + 3], axis=0) for h in range(2)]
            r = dot(wf9[...], jnp.concatenate(cols, axis=1))
            for h in range(2):
                z = 2 * pair + h
                v = parts[z][0:32] + parts[z + 1][32:64] + parts[z + 2][64:96] + r[:, 128 * h : 128 * h + 128]
                v = act(v).astype(BF)
                fine[k, z] = v
                rows.append(v)
        left = []
        for p in range(7):
            for b in range(2):
                left.append(jnp.concatenate([rows[4 * p + b], rows[4 * p + 2 + b]], axis=1))
        s = dot(jnp.concatenate(left, axis=0), s_fine[...]).astype(BF)
        for i in range(14):
            for c in range(2):
                halves[k, i // 2, (2 * (i % 2) + c) * 32 : (2 * (i % 2) + c) * 32 + 32] = s[
                    32 * i : 32 * i + 32, 128 * c : 128 * c + 128
                ]
        return carry

    lax.fori_loop(0, r_fine.count, fine_conv, 0, unroll=2)

    lane = lax.broadcasted_iota(jnp.int32, (64, 128), 1)

    need(wd1)

    def middle_in(k, carry):
        direct = [[], []]
        for p in range(7):
            cols = []
            for h in range(2):
                rel = 2 * (2 * k + h + r_mid.low)
                cols.append(jnp.concatenate([halves[r_fine.at(rel + a), p] for a in range(2)], axis=0))
            r = act(dot(wd1[...], jnp.concatenate(cols, axis=1)))
            for h in range(2):
                direct[h].append(r[:, 128 * h : 128 * h + 128])
        for h in range(2):
            turned = [pltpu.roll(v, 64, 1) for v in direct[h]]
            for pos in range(13):
                p = pos // 2
                v = direct[h][p] if pos % 2 == 0 else jnp.where(lane < 64, turned[p], turned[p + 1])
                low, high = shifted_64(v, lane)
                for dx, u in enumerate((low, v, high)):
                    at = pos * 192 + dx * 64
                    lifted[2 * k + h, at : at + 64] = u.astype(BF)
        return carry

    lax.fori_loop(0, r_mid.count // 2, middle_in, 0)

    need(wm)

    def middle_conv(k, carry):
        parts = []
        start = pl.multiple_of(k * 384, 384)
        for pair in range(r_mid.count // 2):
            cols = [lifted[2 * pair + h, pl.ds(start, 576)] for h in range(2)]
            r = dot(wm[...], jnp.concatenate(cols, axis=1))
            parts += [r[:, :128], r[:, 128:]]
        for y in range(r_skip.count):
            rel = y + r_skip.low
            v = sum(parts[r_mid.at(rel + dy - 1)][64 * dy : 64 * dy + 64] for dy in range(3))
            mskip[y, k] = act(v).astype(BF)
        return carry

    lax.fori_loop(0, 6, middle_conv, 0)

    need(s_mid, wd2, s_taps)

    for chunk in range(2):
        width = 4 if chunk == 0 else 2
        left = [
            jnp.concatenate([mskip[y, 4 * chunk + q] for q in range(width)], axis=1) for y in range(r_skip.count)
        ]
        s = dot(jnp.concatenate(left, axis=0), s_mid[: 128 * width]).astype(BF)
        for y in range(r_skip.count):
            for t in range(4):
                quarters[y, t * 64 : t * 64 + 64, 128 * chunk : 128 * chunk + 128] = s[
                    64 * y : 64 * y + 64, 128 * t : 128 * t + 128
                ]
    for y in range(r_coarse.count):
        rel = 2 * (y + r_coarse.low)
        right = jnp.concatenate([quarters[r_skip.at(rel + a)] for a in range(2)], axis=0)
        cin = act(dot(wd2[...], right)).astype(BF)
        taps = dot(cin, s_taps[...]).astype(BF)
        for t in range(9):
            ctaps[y, 128 * t : 128 * t + 128] = taps[:, 128 * t : 128 * t + 128]

    need(ck, we2, s_mid_t)

    wc = jnp.concatenate([ck[t] for t in range(27)], axis=1)
    for first in (-1, 1):
        rels = (first, first + 1) if first < 1 else (first, first)
        cols = [jnp.concatenate([ctaps[r_coarse.at(rel + dy)] for dy in (-1, 0, 1)], axis=0) for rel in rels]
        cout = act(dot(wc, jnp.concatenate(cols, axis=1))).astype(BF)
        u = act(dot(we2[...], cout)).astype(BF)
        for h in range(2 if first < 1 else 1):
            for a in range(2):
                left = jnp.concatenate(
                    [u[(4 * a + t) * 64 : (4 * a + t) * 64 + 64, 128 * h : 128 * h + 128] for t in range(4)], axis=1
                )
                s = dot(left, s_mid_t[...]).astype(BF)
                for q in range(4):
                    ups[2 * (first + 1 + h) + a, q] = s[:, 128 * q : 128 * q + 128]

    need(mmk)

    lane128 = lax.broadcasted_iota(jnp.int32, (128, 128), 1)
    for y in range(6):
        direct = [
            jnp.concatenate([ups[y, q], mskip[r_skip.at(y - 2), q + 1]], axis=0).astype(F32) for q in range(4)
        ]
        turned = [pltpu.roll(v, 64, 1) for v in direct]
        for pos in range(7):
            p = pos // 2
            v = direct[p] if pos % 2 == 0 else jnp.where(lane128 < 64, turned[p], turned[p + 1])
            low, high = shifted_64(v, lane128)
            for dx, u in enumerate((low, v, high)):
                at = pos * 384 + dx * 128
                joined[y, at : at + 128] = u.astype(BF)
    wmm = jnp.concatenate(
        [
            jnp.concatenate([mmk[9 * dy + 3 * dz + dx] for dz in range(3) for dx in range(3)], axis=1)
            for dy in range(3)
        ],
        axis=0,
    )
    for k in range(3):
        parts = []
        for pair in range(3):
            cols = [joined[2 * pair + h, 768 * k : 768 * k + 1152] for h in range(2)]
            r = dot(wmm, jnp.concatenate(cols, axis=1))
            parts += [r[:, :128], r[:, 128:]]
        for y in range(4):
            v = parts[y][0:64] + parts[y + 1][64:128] + parts[y + 2][128:192]
            mout[y, k] = act(v).astype(BF)

    need(we1, s_fine_t)

    for y in range(4):
        for k in range(3):
            u = act(dot(we1[...], mout[y, k])).astype(BF)
            left = []
            for ab in range(4):
                left.append(jnp.concatenate([u[64 * ab : 64 * ab + 32], u[64 * ab + 32 : 64 * ab + 64]], axis=1))
            s = dot(jnp.concatenate(left, axis=0), s_fine_t[...])
            for a in range(2):
                yf = 2 * (y - 1) + a
                if not -1 <= yf <= 4:
                    continue
                for b in range(2):
                    for h in range(2):
                        zf = -2 + 4 * k + 2 * h + b
                        if not -1 <= zf <= 8:
                            continue
                        up = s[(2 * a + b) * 32 : (2 * a + b) * 32 + 32, 128 * h : 128 * h + 128]
                        skip = fine[r_fine.at(yf), zf + 10].astype(F32)
                        v = jnp.concatenate([up, skip], axis=0)
                        lifted[yf + 1, 192 * (zf + 1) + 0 : 192 * (zf + 1) + 64] = pltpu.roll(v, 1, 1).astype(BF)
                        lifted[yf + 1, 192 * (zf + 1) + 64 : 192 * (zf + 1) + 128] = v.astype(BF)
                        lifted[yf + 1, 192 * (zf + 1) + 128 : 192 * (zf + 1) + 192] = pltpu.roll(v, 127, 1).astype(BF)

    need(wmf)

    for y in range(4):
        parts = []
        for pair in range(5):
            cols = [jnp.concatenate([lifted[y + dy, 192 * (2 * pair + h) : 192 * (2 * pair + h) + 192] for dy in range(3)], axis=0) for h in range(2)]
            r = dot(wmf[...], jnp.concatenate(cols, axis=1))
            parts += [r[:, :128], r[:, 128:]]
        rows = []
        for z in range(8):
            v = parts[z][0:32] + parts[z + 1][32:64] + parts[z + 2][64:96]
            rows.append(act(v).astype(BF))
        d = dot(head[...], jnp.concatenate(rows, axis=1))
        for z in range(8):
            for o in range(3):
                out[o, y, z : z + 1, :] = d[o : o + 1, 128 * z : 128 * z + 128]


def ring(axis, hops):
    count = lax.axis_size(axis)
    return [(i, (i + hops) % count) for i in range(count)]


def body(
    linear_field,
    lift_kernel,
    fine_kernel,
    reduce_first,
    middle_kernel,
    reduce_second,
    coarse_kernel,
    expand_second,
    merge_middle,
    expand_first,
    merge_fine,
    output_head,
):
    raw = [
        fine_kernel,
        reduce_first.transpose(0, 2, 1).reshape(256, 64),
        middle_kernel,
        reduce_second.transpose(0, 2, 1).reshape(512, 128),
        merge_fine,
    ]
    forms = [
        (256, 432),
        (96, 256),
        (32, 96),
        (64, 256),
        (192, 576),
        (128, 512),
        (96, 576),
        (256, 256),
        (256, 256),
        (512, 512),
        (512, 512),
        (256, 1152),
    ]
    prepared = pl.pallas_call(
        prep_kernel,
        out_shape=[jax.ShapeDtypeStruct(s, BF) for s in forms],
        in_specs=[VMEM] + [HBM] * len(raw),
        out_specs=[HBM] * len(forms),
        scratch_shapes=[pltpu.VMEM(s, BF) for s in forms]
        + [pltpu.VMEM(w.shape, BF) for w in raw]
        + [pltpu.SemaphoreType.DMA((len(raw),)), pltpu.SemaphoreType.DMA((len(forms),))],
        cost_estimate=pl.CostEstimate(flops=4_000_000_000, bytes_accessed=10_000_000, transcendentals=0),
        compiler_params=pltpu.CompilerParams(vmem_limit_bytes=60 << 20),
    )(lift_kernel.transpose(2, 0, 1), *raw)
    count_y, count_z = lax.axis_size("gy"), lax.axis_size("gz")
    periodic = count_y == 4
    if periodic:
        own = lax.all_gather(linear_field, "gy")
        sides = []
        for hops in (1, 2):
            pairs = []
            for y in range(count_y):
                step = -hops if y % 2 == 0 else hops
                pairs += [(y * count_z + (z + step) % count_z, y * count_z + z) for z in range(count_z)]
            sides.append(lax.ppermute(own, ("gy", "gz"), pairs))
        *sides, prepared = lax.optimization_barrier((*sides, prepared))
        swap = [(y, y + 1 - 2 * (y % 2)) for y in range(count_y)]
        fields = [own, *sides, *(lax.ppermute(side, "gy", swap) for side in sides)]
    else:
        send = functools.partial(lax.ppermute, axis_name="gz")
        below = send(linear_field, perm=ring("gz", 1))
        above = send(linear_field, perm=ring("gz", -1))
        below_2 = send(linear_field[:, :, 4:], perm=ring("gz", 2))
        above_2 = send(linear_field[:, :, :4], perm=ring("gz", -2))
        wide = jnp.concatenate([below_2, below, linear_field, above, above_2], axis=2)
        fields = [
            jnp.stack([wide if h == 0 else lax.ppermute(wide, "gy", ring("gy", -h)) for h in range(-3, 4)])
        ]
    me = lax.axis_index("gy").astype(jnp.int32).reshape(1)

    t_w, wf, wf9, wd1, wm, wd2, wmf, split_f, split_ft, split_m, split_mt, taps = prepared

    r_lin, r_lift, r_fine, r_mid, r_skip, r_coarse = levels(periodic)
    scratch = [
        pltpu.VMEM((r_lin.count, 4, 144, 128), BF),
        pltpu.VMEM((r_lift.count, 30 * 96, 128), BF),
        pltpu.VMEM((r_fine.count, 28, 32, 128), BF),
        pltpu.VMEM((r_fine.count, 7, 128, 128), BF),
        pltpu.VMEM((r_skip.count, 6, 64, 128), BF),
        pltpu.VMEM((r_skip.count, 256, 256), BF),
        pltpu.VMEM((r_coarse.count, 1152, 128), BF),
        pltpu.VMEM((6, 4, 64, 128), BF),
        pltpu.VMEM((4, 3, 64, 128), BF),
        pltpu.VMEM((6, 7 * 384, 128), BF),
    ]
    weights = [
        t_w,
        wf,
        wf9,
        wd1,
        wm,
        wd2,
        coarse_kernel,
        expand_second.reshape(512, 128),
        merge_middle,
        expand_first.reshape(256, 64),
        wmf,
        split_f,
        split_ft,
        split_m,
        split_mt,
        taps,
    ]
    scratch += [pltpu.VMEM(w.shape, BF) for w in weights]
    scratch.append(pltpu.SemaphoreType.DMA((len(weights),)))
    scratch += [pltpu.VMEM(f.shape, BF) for f in fields] + [pltpu.SemaphoreType.DMA((len(fields),))]
    return pl.pallas_call(
        functools.partial(net_kernel, periodic),
        out_shape=jax.ShapeDtypeStruct(linear_field.shape, F32),
        in_specs=[SMEM] + [ANY] * len(fields) + [VMEM] + [HBM] * len(weights),
        out_specs=VMEM,
        scratch_shapes=scratch,
        compiler_params=pltpu.CompilerParams(vmem_limit_bytes=60 << 20),
    )(me, *fields, output_head, *weights)


def solution(mesh):
    return jax.shard_map(
        body,
        mesh=mesh,
        in_specs=(P(None, "gy", "gz", None), P(), P(), P(), P(), P(), P(), P(), P(), P(), P(), P()),
        out_specs=P(None, "gy", "gz", None),
        check_vma=False,
    )
```

```python
import functools

import jax
import jax.numpy as jnp
from jax import lax
from jax.experimental import pallas as pl
from jax.experimental.pallas import tpu as pltpu
from jax.sharding import PartitionSpec as P

BF = jnp.bfloat16
F32 = jnp.float32
VMEM = pl.BlockSpec(memory_space=pltpu.VMEM)
ANY = pl.BlockSpec(memory_space=pl.ANY)
HBM = pl.BlockSpec(memory_space=pltpu.HBM)
SMEM = pl.BlockSpec(memory_space=pltpu.SMEM)


def act(values):
    return jnp.maximum(values, 0.1 * values)


def dot(left, right):
    return jnp.dot(left, right, preferred_element_type=F32)


def iotas(rows, columns):
    return (
        lax.broadcasted_iota(jnp.int32, (rows, columns), 0),
        lax.broadcasted_iota(jnp.int32, (rows, columns), 1),
    )


def chosen(test):
    return jnp.where(test, 1.0, 0.0).astype(BF)


def fine_order(i):
    return ((i & 1) << 7) | ((i >> 7) << 6) | ((i & 127) >> 1)


def middle_order(i):
    return (((i >> 6) & 1) << 8) | ((i & 1) << 7) | ((i >> 7) << 5) | ((i & 63) >> 1)


def coarse_tap(dz, dx):
    r, c = iotas(256, 128)
    return chosen(r == ((((c >> 5) + dz) << 5) | ((c + dx - 1) & 31)))


def lift_spread(c):
    r, col = iotas(27, 512)
    return chosen(col == ((r // 9 * 3 + c) * 3 + r % 3) * 16 + r // 3 % 3)


def prep_kernel(lift, *refs):
    sources, refs = refs[:5], refs[5:]
    results, refs = refs[:13], refs[13:]
    (t_o, wf_o, wf9_o, wd1_o, wm_o, wm9_o, wd2_o, wmf_o, sf_o, sft_o, sm_o, smt_o, st_o), refs = refs[:13], refs[13:]
    (fine, red1, mid, red2, mfine), sems, out_sems = refs[:5], refs[5], refs[6]
    copies = [pltpu.make_async_copy(src, dst, sems.at[i]) for i, (src, dst) in enumerate(zip(sources, refs))]
    for copy in copies:
        copy.start()
    r, c = iotas(256, 256)
    sf_o[...] = chosen(fine_order(r) == c)
    sft_o[...] = chosen(r == fine_order(c))
    r, c = iotas(512, 512)
    sm_o[...] = chosen(middle_order(r) == c)
    smt_o[...] = chosen(r == middle_order(c))
    for t in range(9):
        st_o[:, 128 * t : 128 * t + 128] = coarse_tap(t // 3, t % 3)
    base = sum(
        lax.dot_general(lift[c], lift_spread(c), (((0,), (0,)), ((), ())), preferred_element_type=F32)
        for c in range(3)
    )
    for zo in range(8):
        moved = base if zo == 0 else pltpu.roll(base, zo, 1)
        t_o[32 * zo : 32 * zo + 32] = moved[:, :432].astype(BF)
    for copy in copies:
        copy.wait()
    wf9_o[...] = jnp.zeros_like(wf9_o)
    for dz in range(3):
        for dy in range(3):
            for dx in range(3):
                k = 3 * dy + dx
                if k < 8:
                    wf_o[32 * dz : 32 * dz + 32, 32 * k : 32 * k + 32] = fine[9 * dy + 3 * dz + dx]
                else:
                    for zo in range(2):
                        wf9_o[32 * zo : 32 * zo + 32, 32 * (dz + zo) : 32 * (dz + zo) + 32] = fine[9 * dy + 3 * dz + dx]
                wmf_o[32 * dz : 32 * dz + 32, 64 * k : 64 * k + 64] = mfine[9 * dy + 3 * dz + dx]
                j = 3 * dz + dx
                if j < 8:
                    wm_o[64 * dy : 64 * dy + 64, 64 * j : 64 * j + 64] = mid[9 * dy + 3 * dz + dx]
                else:
                    wm9_o[:, 64 * dy : 64 * dy + 64] = mid[9 * dy + 3 * dz + dx]
    wd1_o[...] = red1[...].astype(F32).T.astype(BF)
    wd2_o[...] = red2[...].astype(F32).T.astype(BF)
    made = (t_o, wf_o, wf9_o, wd1_o, wm_o, wm9_o, wd2_o, wmf_o, sf_o, sft_o, sm_o, smt_o, st_o)
    copies = [pltpu.make_async_copy(src, dst, out_sems.at[i]) for i, (src, dst) in enumerate(zip(made, results))]
    for copy in copies:
        copy.start()
    for copy in copies:
        copy.wait()


class Rows:
    def __init__(self, low, count, periodic):
        self.low, self.count, self.periodic = low, count, periodic

    def at(self, rel):
        if self.periodic:
            moved = rel - self.low + 4 * self.count
            return moved % self.count if isinstance(moved, int) else lax.rem(moved, self.count)
        return rel - self.low


def levels(periodic):
    if periodic:
        fine, mid, coarse = Rows(-8, 16, True), Rows(-4, 8, True), Rows(-2, 4, True)
        return fine, fine, fine, mid, mid, coarse
    return (
        Rows(-12, 28, False),
        Rows(-11, 26, False),
        Rows(-10, 24, False),
        Rows(-5, 12, False),
        Rows(-4, 10, False),
        Rows(-2, 5, False),
    )


def shifted_rows(direct):
    lane = lax.broadcasted_iota(jnp.int32, direct[0].shape, 1)
    first = lane < 64
    edges = (lane & 63) == 0, (lane & 63) == 63
    kept, swapped = [], []
    for v in direct:
        t = pltpu.roll(v, 64, 1)
        pairs = [(pltpu.roll(v, n, 1), pltpu.roll(t, n, 1)) for n in (1, 127)]
        low, high = (jnp.where(edge, rt, rv) for edge, (rv, rt) in zip(edges, pairs))
        low_t, high_t = (jnp.where(edge, rv, rt) for edge, (rv, rt) in zip(edges, pairs))
        kept.append((low, v, high))
        swapped.append((low_t, t, high_t))
    result = []
    for p in range(len(direct)):
        result.append(kept[p])
        if p + 1 < len(direct):
            result.append(tuple(jnp.where(first, u, w) for u, w in zip(swapped[p], swapped[p + 1])))
    return result


def net_kernel(periodic, me, *refs):
    count = 5 if periodic else 1
    fields, refs = refs[:count], refs[count:]
    head, weights, out, refs = refs[0], refs[1:18], refs[18], refs[19:]
    pat, lifted, fine, halves, mskip, quarters, ctaps, ups, mout, joined = refs[:10]
    held, sems = refs[10:27], refs[27]
    near_by, field_sems = refs[28 : 28 + count], refs[28 + count]
    field_copies = [
        pltpu.make_async_copy(src, dst, field_sems.at[i]) for i, (src, dst) in enumerate(zip(fields, near_by))
    ]
    for copy in field_copies:
        copy.start()
    copies = [pltpu.make_async_copy(src, dst, sems.at[i]) for i, (src, dst) in enumerate(zip(weights, held))]
    copies[0].start()
    if periodic:
        own, near, far, other_near, other_far = near_by
    else:
        wide = near_by[0]
    (t_w, wf, wf9, s_fine, wd1, wm, wm9, s_mid, wd2, s_taps, ck, we2, s_mid_t, mmk, we1, s_fine_t, wmf) = held

    def need(*names):
        for name in names:
            copies[[h is name for h in held].index(True)].wait()

    r_lin, r_lift, r_fine, r_mid, r_skip, r_coarse = levels(periodic)
    core = lax.rem(me[0], 2)

    for copy in field_copies:
        copy.wait()

    def patch(k, carry):
        row = lax.rem(k, 4)
        if periodic:
            block = lax.rem(me[0] + k // 4 + 2, 4)
        for c in range(3):
            if periodic:
                mine = [ref[block, c, row].astype(F32) for ref in (near, far)]
                others = [ref[block, c, row].astype(F32) for ref in (other_near, other_far)]
                below_1, below_2 = (jnp.where(core == 0, m, t) for m, t in zip(mine, others))
                above_1, above_2 = (jnp.where(core == 0, t, m) for m, t in zip(mine, others))
                parts = [below_2[4:], below_1, own[block, c, row].astype(F32), above_1, above_2[:4]]
                mid_v = jnp.concatenate(parts, axis=0)
            else:
                mid_v = wide[k // 4, c, row].astype(F32)
            for dx, v in enumerate((pltpu.roll(mid_v, 1, 1), mid_v, pltpu.roll(mid_v, 127, 1))):
                v = jnp.concatenate([v, jnp.zeros((8, 128), F32)], axis=0)
                for j in range(4):
                    pat[k, j, (3 * c + dx) * 16 : (3 * c + dx) * 16 + 16] = v[8 * j : 8 * j + 16].astype(BF)
        return carry

    lax.fori_loop(0, r_lin.count, patch, 0, unroll=8)
    for copy in copies[1:]:
        copy.start()

    need(t_w)

    def lift(k, carry):
        rel = k + r_lift.low
        ys = [r_lin.at(rel + dy) for dy in (-1, 0, 1)]
        for pair in range(2):
            cols = [jnp.concatenate([pat[y, 2 * pair + h] for y in ys], axis=0) for h in range(2)]
            r = act(dot(t_w[...], jnp.concatenate(cols, axis=1)))
            for h in range(2):
                for zo in range(8):
                    z = 16 * pair + 8 * h + zo
                    if z < 30:
                        v = r[32 * zo : 32 * zo + 32, 128 * h : 128 * h + 128]
                        lifted[k, 96 * z : 96 * z + 32] = pltpu.roll(v, 1, 1).astype(BF)
                        lifted[k, 96 * z + 32 : 96 * z + 64] = v.astype(BF)
                        lifted[k, 96 * z + 64 : 96 * z + 96] = pltpu.roll(v, 127, 1).astype(BF)
        return carry

    lax.fori_loop(0, r_lift.count, lift, 0, unroll=8)

    need(wf, wf9, s_fine)

    def fine_conv(k, carry):
        rel = k + r_fine.low
        ys = [r_lift.at(rel + dy) for dy in (-1, 0, 1)]
        parts = []
        for pair in range(15):
            cols = [
                jnp.concatenate([*(lifted[y, 96 * (2 * pair + h) : 96 * (2 * pair + h) + 96] for y in ys[:2]), lifted[ys[2], 96 * (2 * pair + h) : 96 * (2 * pair + h) + 64]], axis=0)
                for h in range(2)
            ]
            r = dot(wf[...], jnp.concatenate(cols, axis=1))
            parts += [r[:, :128], r[:, 128:]]
        rows = []
        last = [lifted[ys[2], 96 * z + 64 : 96 * z + 96] for z in range(30)]
        for quad in range(7):
            cols = [jnp.concatenate(last[4 * quad + 2 * h : 4 * quad + 2 * h + 4], axis=0) for h in range(2)]
            r = dot(wf9[...], jnp.concatenate(cols, axis=1))
            for i in range(4):
                z, zo, h = 4 * quad + i, i % 2, i // 2
                v = parts[z][0:32] + parts[z + 1][32:64] + parts[z + 2][64:96]
                v = act(v + r[32 * zo : 32 * zo + 32, 128 * h : 128 * h + 128]).astype(BF)
                fine[k, z] = v
                rows.append(v)
        left = []
        for p in range(7):
            for b in range(2):
                left.append(jnp.concatenate([rows[4 * p + b], rows[4 * p + 2 + b]], axis=1))
        s = dot(jnp.concatenate(left, axis=0), s_fine[...]).astype(BF)
        for i in range(14):
            for c in range(2):
                halves[k, i // 2, (2 * (i % 2) + c) * 32 : (2 * (i % 2) + c) * 32 + 32] = s[
                    32 * i : 32 * i + 32, 128 * c : 128 * c + 128
                ]
        return carry

    lax.fori_loop(0, r_fine.count, fine_conv, 0, unroll=8)

    need(wd1)

    def middle_in(k, carry):
        direct = [[], []]
        for p in range(7):
            cols = []
            for h in range(2):
                rel = 2 * (2 * k + h + r_mid.low)
                cols.append(jnp.concatenate([halves[r_fine.at(rel + a), p] for a in range(2)], axis=0))
            r = act(dot(wd1[...], jnp.concatenate(cols, axis=1)))
            for h in range(2):
                direct[h].append(r[:, 128 * h : 128 * h + 128])
        for h in range(2):
            for pos, triple in enumerate(shifted_rows(direct[h])):
                for dx, u in enumerate(triple):
                    at = pos * 192 + dx * 64
                    lifted[2 * k + h, at : at + 64] = u.astype(BF)
        return carry

    lax.fori_loop(0, r_mid.count // 2, middle_in, 0)

    need(wm, wm9)

    def middle_conv(k, carry):
        parts = []
        start = pl.multiple_of(k * 384, 384)
        for pair in range(r_mid.count // 2):
            cols = [lifted[2 * pair + h, pl.ds(start, 512)] for h in range(2)]
            r = dot(wm[...], jnp.concatenate(cols, axis=1))
            parts += [r[:, :128], r[:, 128:]]
        last = [lifted[y, pl.ds(start + 512, 64)] for y in range(r_mid.count)]
        for pair in range(r_skip.count // 2):
            rels = [2 * pair + h + r_skip.low for h in range(2)]
            cols = [jnp.concatenate([last[r_mid.at(rel + dy)] for dy in (-1, 0, 1)], axis=0) for rel in rels]
            r = dot(wm9[...], jnp.concatenate(cols, axis=1))
            for h, rel in enumerate(rels):
                v = sum(parts[r_mid.at(rel + dy - 1)][64 * dy : 64 * dy + 64] for dy in range(3))
                mskip[2 * pair + h, k] = act(v + r[:, 128 * h : 128 * h + 128]).astype(BF)
        return carry

    lax.fori_loop(0, 6, middle_conv, 0, unroll=True)

    need(s_mid, wd2, s_taps)

    for chunk in range(2):
        width = 4 if chunk == 0 else 2
        left = [
            jnp.concatenate([mskip[y, 4 * chunk + q] for q in range(width)], axis=1) for y in range(r_skip.count)
        ]
        s = dot(jnp.concatenate(left, axis=0), s_mid[: 128 * width]).astype(BF)
        for y in range(r_skip.count):
            for t in range(4):
                quarters[y, t * 64 : t * 64 + 64, 128 * chunk : 128 * chunk + 128] = s[
                    64 * y : 64 * y + 64, 128 * t : 128 * t + 128
                ]
    cin = []
    for y in range(r_coarse.count):
        rel = 2 * (y + r_coarse.low)
        right = jnp.concatenate([quarters[r_skip.at(rel + a)] for a in range(2)], axis=0)
        cin.append(act(dot(wd2[...], right)).astype(BF))
    taps = dot(jnp.concatenate(cin, axis=0), s_taps[...]).astype(BF)
    for y in range(r_coarse.count):
        for t in range(9):
            ctaps[y, 128 * t : 128 * t + 128] = taps[128 * y : 128 * y + 128, 128 * t : 128 * t + 128]

    need(ck, we2, s_mid_t)

    wc = jnp.concatenate([ck[t] for t in range(27)], axis=1)
    for first in (-1, 1):
        rels = (first, first + 1) if first < 1 else (first, first)
        cols = [jnp.concatenate([ctaps[r_coarse.at(rel + dy)] for dy in (-1, 0, 1)], axis=0) for rel in rels]
        cout = act(dot(wc, jnp.concatenate(cols, axis=1))).astype(BF)
        u = act(dot(we2[...], cout)).astype(BF)
        rows = []
        for h in range(2 if first < 1 else 1):
            for a in range(2):
                blocks = [u[(4 * a + t) * 64 : (4 * a + t) * 64 + 64, 128 * h : 128 * h + 128] for t in range(4)]
                rows.append(jnp.concatenate(blocks, axis=1))
        s = dot(jnp.concatenate(rows, axis=0), s_mid_t[...]).astype(BF)
        for i in range(len(rows)):
            for q in range(4):
                ups[2 * (first + 1) + i, q] = s[64 * i : 64 * i + 64, 128 * q : 128 * q + 128]

    need(mmk)

    for y in range(6):
        direct = [
            jnp.concatenate([ups[y, q], mskip[r_skip.at(y - 2), q + 1]], axis=0).astype(F32) for q in range(4)
        ]
        for pos, triple in enumerate(shifted_rows(direct)):
            for dx, u in enumerate(triple):
                at = pos * 384 + dx * 128
                joined[y, at : at + 128] = u.astype(BF)
    wmm = jnp.concatenate(
        [
            jnp.concatenate([mmk[9 * dy + 3 * dz + dx] for dz in range(3) for dx in range(3)], axis=1)
            for dy in range(3)
        ],
        axis=0,
    )
    for k in range(3):
        parts = []
        for pair in range(3):
            cols = [joined[2 * pair + h, 768 * k : 768 * k + 1152] for h in range(2)]
            r = dot(wmm, jnp.concatenate(cols, axis=1))
            parts += [r[:, :128], r[:, 128:]]
        for y in range(4):
            v = parts[y][0:64] + parts[y + 1][64:128] + parts[y + 2][128:192]
            mout[y, k] = act(v).astype(BF)

    need(we1, s_fine_t)

    for y in range(4):
        for k in range(3):
            u = act(dot(we1[...], mout[y, k])).astype(BF)
            left = []
            for ab in range(4):
                left.append(jnp.concatenate([u[64 * ab : 64 * ab + 32], u[64 * ab + 32 : 64 * ab + 64]], axis=1))
            s = dot(jnp.concatenate(left, axis=0), s_fine_t[...])
            for a in range(2):
                yf = 2 * (y - 1) + a
                if not -1 <= yf <= 4:
                    continue
                for b in range(2):
                    for h in range(2):
                        zf = -2 + 4 * k + 2 * h + b
                        if not -1 <= zf <= 8:
                            continue
                        up = s[(2 * a + b) * 32 : (2 * a + b) * 32 + 32, 128 * h : 128 * h + 128]
                        skip = fine[r_fine.at(yf), zf + 10].astype(F32)
                        v = jnp.concatenate([up, skip], axis=0)
                        lifted[yf + 1, 192 * (zf + 1) + 0 : 192 * (zf + 1) + 64] = pltpu.roll(v, 1, 1).astype(BF)
                        lifted[yf + 1, 192 * (zf + 1) + 64 : 192 * (zf + 1) + 128] = v.astype(BF)
                        lifted[yf + 1, 192 * (zf + 1) + 128 : 192 * (zf + 1) + 192] = pltpu.roll(v, 127, 1).astype(BF)

    need(wmf)

    for y in range(4):
        parts = []
        for pair in range(5):
            cols = [jnp.concatenate([lifted[y + dy, 192 * (2 * pair + h) : 192 * (2 * pair + h) + 192] for dy in range(3)], axis=0) for h in range(2)]
            r = dot(wmf[...], jnp.concatenate(cols, axis=1))
            parts += [r[:, :128], r[:, 128:]]
        rows = []
        for z in range(8):
            v = parts[z][0:32] + parts[z + 1][32:64] + parts[z + 2][64:96]
            rows.append(act(v).astype(BF))
        d = dot(head[...], jnp.concatenate(rows, axis=1))
        for z in range(8):
            for o in range(3):
                out[o, y, z : z + 1, :] = d[o : o + 1, 128 * z : 128 * z + 128]


def ring(axis, hops):
    count = lax.axis_size(axis)
    return [(i, (i + hops) % count) for i in range(count)]


def body(
    linear_field,
    lift_kernel,
    fine_kernel,
    reduce_first,
    middle_kernel,
    reduce_second,
    coarse_kernel,
    expand_second,
    merge_middle,
    expand_first,
    merge_fine,
    output_head,
):
    raw = [
        fine_kernel,
        reduce_first.transpose(0, 2, 1).reshape(256, 64),
        middle_kernel,
        reduce_second.transpose(0, 2, 1).reshape(512, 128),
        merge_fine,
    ]
    forms = [
        (256, 432),
        (96, 256),
        (64, 128),
        (64, 256),
        (192, 512),
        (64, 192),
        (128, 512),
        (96, 576),
        (256, 256),
        (256, 256),
        (512, 512),
        (512, 512),
        (256, 1152),
    ]
    prepared = pl.pallas_call(
        prep_kernel,
        out_shape=[jax.ShapeDtypeStruct(s, BF) for s in forms],
        in_specs=[VMEM] + [HBM] * len(raw),
        out_specs=[HBM] * len(forms),
        scratch_shapes=[pltpu.VMEM(s, BF) for s in forms]
        + [pltpu.VMEM(w.shape, BF) for w in raw]
        + [pltpu.SemaphoreType.DMA((len(raw),)), pltpu.SemaphoreType.DMA((len(forms),))],
        cost_estimate=pl.CostEstimate(flops=4_000_000_000, bytes_accessed=10_000_000, transcendentals=0),
        compiler_params=pltpu.CompilerParams(vmem_limit_bytes=60 << 20),
    )(lift_kernel.transpose(2, 0, 1), *raw)
    count_y, count_z = lax.axis_size("gy"), lax.axis_size("gz")
    periodic = count_y == 4
    if periodic:
        own = lax.all_gather(linear_field, "gy")
        sides = []
        for hops in (1, 2):
            pairs = []
            for y in range(count_y):
                step = -hops if y % 2 == 0 else hops
                pairs += [(y * count_z + (z + step) % count_z, y * count_z + z) for z in range(count_z)]
            sides.append(lax.ppermute(own, ("gy", "gz"), pairs))
        *sides, prepared = lax.optimization_barrier((*sides, prepared))
        swap = [(y, y + 1 - 2 * (y % 2)) for y in range(count_y)]
        fields = [own, *sides, *(lax.ppermute(side, "gy", swap) for side in sides)]
    else:
        send = functools.partial(lax.ppermute, axis_name="gz")
        below = send(linear_field, perm=ring("gz", 1))
        above = send(linear_field, perm=ring("gz", -1))
        below_2 = send(linear_field[:, :, 4:], perm=ring("gz", 2))
        above_2 = send(linear_field[:, :, :4], perm=ring("gz", -2))
        wide = jnp.concatenate([below_2, below, linear_field, above, above_2], axis=2)
        fields = [
            jnp.stack([wide if h == 0 else lax.ppermute(wide, "gy", ring("gy", -h)) for h in range(-3, 4)])
        ]
    me = lax.axis_index("gy").astype(jnp.int32).reshape(1)

    t_w, wf, wf9, wd1, wm, wm9, wd2, wmf, split_f, split_ft, split_m, split_mt, taps = prepared

    r_lin, r_lift, r_fine, r_mid, r_skip, r_coarse = levels(periodic)
    scratch = [
        pltpu.VMEM((r_lin.count, 4, 144, 128), BF),
        pltpu.VMEM((r_lift.count, 30 * 96, 128), BF),
        pltpu.VMEM((r_fine.count, 28, 32, 128), BF),
        pltpu.VMEM((r_fine.count, 7, 128, 128), BF),
        pltpu.VMEM((r_skip.count, 6, 64, 128), BF),
        pltpu.VMEM((r_skip.count, 256, 256), BF),
        pltpu.VMEM((r_coarse.count, 1152, 128), BF),
        pltpu.VMEM((6, 4, 64, 128), BF),
        pltpu.VMEM((4, 3, 64, 128), BF),
        pltpu.VMEM((6, 7 * 384, 128), BF),
    ]
    weights = [
        t_w,
        wf,
        wf9,
        split_f,
        wd1,
        wm,
        wm9,
        split_m,
        wd2,
        taps,
        coarse_kernel,
        expand_second.reshape(512, 128),
        split_mt,
        merge_middle,
        expand_first.reshape(256, 64),
        split_ft,
        wmf,
    ]
    scratch += [pltpu.VMEM(w.shape, BF) for w in weights]
    scratch.append(pltpu.SemaphoreType.DMA((len(weights),)))
    scratch += [pltpu.VMEM(f.shape, BF) for f in fields] + [pltpu.SemaphoreType.DMA((len(fields),))]
    return pl.pallas_call(
        functools.partial(net_kernel, periodic),
        out_shape=jax.ShapeDtypeStruct(linear_field.shape, F32),
        in_specs=[SMEM] + [ANY] * len(fields) + [VMEM] + [HBM] * len(weights),
        out_specs=VMEM,
        scratch_shapes=scratch,
        compiler_params=pltpu.CompilerParams(vmem_limit_bytes=60 << 20),
    )(me, *fields, output_head, *weights)


def solution(mesh):
    return jax.shard_map(
        body,
        mesh=mesh,
        in_specs=(P(None, "gy", "gz", None), P(), P(), P(), P(), P(), P(), P(), P(), P(), P(), P()),
        out_specs=P(None, "gy", "gz", None),
        check_vma=False,
    )
```

```python
import functools

import jax
import jax.numpy as jnp
from jax import lax
from jax.experimental import pallas as pl
from jax.experimental.pallas import tpu as pltpu
from jax.sharding import PartitionSpec as P

BF = jnp.bfloat16
F32 = jnp.float32
VMEM = pl.BlockSpec(memory_space=pltpu.VMEM)
ANY = pl.BlockSpec(memory_space=pl.ANY)
HBM = pl.BlockSpec(memory_space=pltpu.HBM)
SMEM = pl.BlockSpec(memory_space=pltpu.SMEM)


def act(values):
    return jnp.maximum(values, 0.1 * values)


def dot(left, right):
    return jnp.dot(left, right, preferred_element_type=F32)


def iotas(rows, columns):
    return (
        lax.broadcasted_iota(jnp.int32, (rows, columns), 0),
        lax.broadcasted_iota(jnp.int32, (rows, columns), 1),
    )


def chosen(test):
    return jnp.where(test, 1.0, 0.0).astype(BF)


def fine_order(i):
    return ((i & 1) << 7) | ((i >> 7) << 6) | ((i & 127) >> 1)


def split_middle():
    r, c = iotas(384, 512)
    return chosen((((r & 1) << 8) | (((r >> 7) + 3 * ((r >> 6) & 1)) << 5) | ((r & 63) >> 1)) == c)


def join_middle():
    r, c = iotas(512, 640)
    source = ((2 * ((r >> 5) & 3) + (r >> 8)) << 6) | ((r & 31) << 1) | ((r >> 7) & 1)
    return chosen(source == ((((c >> 7) + 3 * ((c >> 6) & 1)) << 6) | (c & 63)))


def coarse_tap(dz, dx):
    r, c = iotas(256, 128)
    return chosen(r == ((((c >> 5) + dz) << 5) | ((c + dx - 1) & 31)))


def lift_spread(c):
    r, col = iotas(27, 512)
    return chosen(col == ((r // 9 * 3 + c) * 3 + r % 3) * 16 + r // 3 % 3)


def prep_kernel(lift, head, *refs):
    sources, refs = refs[:5], refs[5:]
    results, refs = refs[:15], refs[15:]
    (t_o, wf_o, wf9_o, wd1_o, wm_o, wm9_o, wd2_o, wmf_o, wmf9_o, sf_o, sft_o, sm_o, smt_o, st_o, head_o), refs = refs[:15], refs[15:]
    (fine, red1, mid, red2, mfine), sems, out_sems = refs[:5], refs[5], refs[6]
    copies = [pltpu.make_async_copy(src, dst, sems.at[i]) for i, (src, dst) in enumerate(zip(sources, refs))]
    for copy in copies:
        copy.start()
    r, c = iotas(256, 256)
    sf_o[...] = chosen(fine_order(r) == c)
    sft_o[...] = chosen(r == fine_order(c))
    head_o[...] = jnp.concatenate([head[...].astype(F32), jnp.zeros((13, 32), F32)], axis=0).astype(BF)
    sm_o[...] = split_middle()
    smt_o[...] = join_middle()
    for t in range(9):
        st_o[:, 128 * t : 128 * t + 128] = coarse_tap(t // 3, t % 3)
    base = sum(
        lax.dot_general(lift[c], lift_spread(c), (((0,), (0,)), ((), ())), preferred_element_type=F32)
        for c in range(3)
    )
    for zo in range(8):
        moved = base if zo == 0 else pltpu.roll(base, zo, 1)
        t_o[32 * zo : 32 * zo + 32] = moved[:, :432].astype(BF)
    for copy in copies:
        copy.wait()
    wf9_o[...] = jnp.zeros_like(wf9_o)
    wmf9_o[...] = jnp.zeros_like(wmf9_o)
    for dz in range(3):
        for dy in range(3):
            for dx in range(3):
                k = 3 * dy + dx
                if k < 8:
                    wf_o[32 * dz : 32 * dz + 32, 32 * k : 32 * k + 32] = fine[9 * dy + 3 * dz + dx]
                else:
                    for zo in range(6):
                        wf9_o[32 * zo : 32 * zo + 32, 32 * (dz + zo) : 32 * (dz + zo) + 32] = fine[9 * dy + 3 * dz + dx]
                if k < 8:
                    wmf_o[32 * dz : 32 * dz + 32, 64 * k : 64 * k + 64] = mfine[9 * dy + 3 * dz + dx]
                else:
                    for zo in range(2):
                        at = 64 * (dz + zo)
                        wmf9_o[32 * zo : 32 * zo + 32, at : at + 64] = mfine[9 * dy + 3 * dz + dx]
                j = 3 * dz + dx
                if j < 8:
                    wm_o[64 * dy : 64 * dy + 64, 64 * j : 64 * j + 64] = mid[9 * dy + 3 * dz + dx]
                else:
                    wm9_o[:, 64 * dy : 64 * dy + 64] = mid[9 * dy + 3 * dz + dx]
    wd1_o[...] = red1[...].astype(F32).T.astype(BF)
    wd2_o[...] = red2[...].astype(F32).T.astype(BF)
    made = (t_o, wf_o, wf9_o, wd1_o, wm_o, wm9_o, wd2_o, wmf_o, wmf9_o, sf_o, sft_o, sm_o, smt_o, st_o, head_o)
    copies = [pltpu.make_async_copy(src, dst, out_sems.at[i]) for i, (src, dst) in enumerate(zip(made, results))]
    for copy in copies:
        copy.start()
    for copy in copies:
        copy.wait()


class Rows:
    def __init__(self, low, count, periodic):
        self.low, self.count, self.periodic = low, count, periodic

    def at(self, rel):
        if self.periodic:
            moved = rel - self.low + 4 * self.count
            return moved % self.count if isinstance(moved, int) else lax.rem(moved, self.count)
        return rel - self.low


def levels(periodic):
    if periodic:
        fine, mid, coarse = Rows(-8, 16, True), Rows(-4, 8, True), Rows(-2, 4, True)
        return fine, fine, fine, mid, mid, coarse
    return (
        Rows(-12, 28, False),
        Rows(-11, 26, False),
        Rows(-10, 24, False),
        Rows(-5, 12, False),
        Rows(-4, 10, False),
        Rows(-2, 5, False),
    )


def half_shifts(v):
    lane = lax.broadcasted_iota(jnp.int32, v.shape, 1) & 63
    t = pltpu.roll(v, 64, 1)
    low_v, low_t, high_v, high_t = (pltpu.roll(u, n, 1) for n in (1, 127) for u in (v, t))
    low, high = lane == 0, lane == 63
    return (
        (jnp.where(low, low_t, low_v), v, jnp.where(high, high_t, high_v)),
        (jnp.where(low, low_v, low_t), t, jnp.where(high, high_v, high_t)),
    )


def net_kernel(periodic, *refs):
    count = 5 if periodic else 1
    fields, refs = refs[:count], refs[count:]
    weights, out, refs = refs[:19], refs[19], refs[20:]
    pat, lifted, fine, halves, mskip, quarters, ctaps, ups, mout, joined, jfine = refs[:11]
    held, sems = refs[11:30], refs[30]
    near_by, field_sems = refs[31 : 31 + count], refs[31 + count]
    field_copies = [
        pltpu.make_async_copy(src, dst, field_sems.at[i]) for i, (src, dst) in enumerate(zip(fields, near_by))
    ]
    for copy in field_copies:
        copy.start()
    copies = [pltpu.make_async_copy(src, dst, sems.at[i]) for i, (src, dst) in enumerate(zip(weights, held))]
    copies[0].start()
    if periodic:
        own, near, far, other_near, other_far = near_by
    else:
        wide = near_by[0]
    (t_w, wf, wf9, s_fine, wd1, wm, wm9, s_mid, wd2, s_taps, ck, we2, s_mid_t, mmk, we1, s_fine_t, wmf, wmf9, head) = held

    def need(*names):
        for name in names:
            copies[[h is name for h in held].index(True)].wait()

    r_lin, r_lift, r_fine, r_mid, r_skip, r_coarse = levels(periodic)
    me = lax.axis_index("gy")
    core = lax.rem(me, 2)

    for copy in field_copies:
        copy.wait()

    def patch(k, carry):
        row = lax.rem(k, 4)
        if periodic:
            block = lax.rem(me + k // 4 + 2, 4)
        for c in range(3):
            if periodic:
                mine = [ref[block, c, row].astype(F32) for ref in (near, far)]
                others = [ref[block, c, row].astype(F32) for ref in (other_near, other_far)]
                below_1, below_2 = (jnp.where(core == 0, m, t) for m, t in zip(mine, others))
                above_1, above_2 = (jnp.where(core == 0, t, m) for m, t in zip(mine, others))
                parts = [below_2[4:], below_1, own[block, c, row].astype(F32), above_1, above_2[:4]]
                mid_v = jnp.concatenate(parts, axis=0)
            else:
                mid_v = wide[k // 4, c, row].astype(F32)
            for dx, v in enumerate((pltpu.roll(mid_v, 1, 1), mid_v, pltpu.roll(mid_v, 127, 1))):
                v = jnp.concatenate([v, jnp.zeros((8, 128), F32)], axis=0)
                for j in range(4):
                    pat[k, j, (3 * c + dx) * 16 : (3 * c + dx) * 16 + 16] = v[8 * j : 8 * j + 16].astype(BF)
        return carry

    lax.fori_loop(0, r_lin.count, patch, 0, unroll=8)
    for copy in copies[1:]:
        copy.start()

    need(t_w)

    def lift(k, carry):
        rel = k + r_lift.low
        ys = [r_lin.at(rel + dy) for dy in (-1, 0, 1)]
        for pair in range(2):
            cols = [jnp.concatenate([pat[y, 2 * pair + h] for y in ys], axis=0) for h in range(2)]
            r = act(dot(t_w[...], jnp.concatenate(cols, axis=1)))
            for h in range(2):
                for zo in range(8):
                    z = 16 * pair + 8 * h + zo
                    if z < 30:
                        v = r[32 * zo : 32 * zo + 32, 128 * h : 128 * h + 128]
                        lifted[k, 96 * z : 96 * z + 32] = pltpu.roll(v, 1, 1).astype(BF)
                        lifted[k, 96 * z + 32 : 96 * z + 64] = v.astype(BF)
                        lifted[k, 96 * z + 64 : 96 * z + 96] = pltpu.roll(v, 127, 1).astype(BF)
        return carry

    lax.fori_loop(0, r_lift.count, lift, 0, unroll=8)

    need(wf, wf9, s_fine)

    def fine_conv(k, carry):
        rel = k + r_fine.low
        ys = [r_lift.at(rel + dy) for dy in (-1, 0, 1)]
        parts = []
        for pair in range(15):
            cols = [
                jnp.concatenate([*(lifted[y, 96 * (2 * pair + h) : 96 * (2 * pair + h) + 96] for y in ys[:2]), lifted[ys[2], 96 * (2 * pair + h) : 96 * (2 * pair + h) + 64]], axis=0)
                for h in range(2)
            ]
            r = dot(wf[...], jnp.concatenate(cols, axis=1))
            parts += [r[:, :128], r[:, 128:]]
        rows = []
        last = [lifted[ys[2], 96 * z + 64 : 96 * z + 96] for z in range(30)]
        for first, outs in ((0, 6), (12, 6), (24, 2)):
            cols = [jnp.concatenate(last[first + outs * h : first + outs * h + outs + 2], axis=0) for h in range(2)]
            r = dot(wf9[: 32 * outs, : 32 * outs + 64], jnp.concatenate(cols, axis=1))
            for i in range(2 * outs):
                z, zo, h = first + i, i % outs, i // outs
                v = parts[z][0:32] + parts[z + 1][32:64] + parts[z + 2][64:96]
                v = act(v + r[32 * zo : 32 * zo + 32, 128 * h : 128 * h + 128]).astype(BF)
                fine[k, z] = v
                rows.append(v)
        left = [jnp.concatenate([rows[z], rows[z + 14]], axis=1) for z in range(14)]
        s = dot(jnp.concatenate(left, axis=0), s_fine[...]).astype(BF)
        for i in range(14):
            for c in range(2):
                halves[k, i // 2, (2 * (i % 2) + c) * 32 : (2 * (i % 2) + c) * 32 + 32] = s[
                    32 * i : 32 * i + 32, 128 * c : 128 * c + 128
                ]
        return carry

    lax.fori_loop(0, r_fine.count, fine_conv, 0, unroll=8)

    need(wd1)

    def middle_in(k, carry):
        direct = [[], []]
        for p in range(7):
            cols = []
            for h in range(2):
                rel = 2 * (2 * k + h + r_mid.low)
                cols.append(jnp.concatenate([halves[r_fine.at(rel + a), p] for a in range(2)], axis=0))
            r = act(dot(wd1[...], jnp.concatenate(cols, axis=1)))
            for h in range(2):
                direct[h].append(r[:, 128 * h : 128 * h + 128])
        first = lax.broadcasted_iota(jnp.int32, (64, 128), 1) < 64
        for h in range(2):
            kept, turned = zip(*(half_shifts(v.astype(BF)) for v in direct[h]))
            lows = [*kept, turned[0]]
            highs = [turned[6], *kept]
            for q in range(8):
                for dx in range(3):
                    at = q * 192 + dx * 64
                    lifted[2 * k + h, at : at + 64] = jnp.where(first, lows[q][dx], highs[q][dx])
        return carry

    lax.fori_loop(0, r_mid.count // 2, middle_in, 0)

    need(wm, wm9)

    def middle_conv(k, carry):
        parts = []
        start = pl.multiple_of(k * 192, 192)
        for pair in range(r_mid.count // 2):
            cols = [lifted[2 * pair + h, pl.ds(start, 512)] for h in range(2)]
            r = dot(wm[...], jnp.concatenate(cols, axis=1))
            parts += [r[:, :128], r[:, 128:]]
        last = [lifted[y, pl.ds(start + 512, 64)] for y in range(r_mid.count)]
        for pair in range(r_skip.count // 2):
            rels = [2 * pair + h + r_skip.low for h in range(2)]
            cols = [jnp.concatenate([last[r_mid.at(rel + dy)] for dy in (-1, 0, 1)], axis=0) for rel in rels]
            r = dot(wm9[...], jnp.concatenate(cols, axis=1))
            for h, rel in enumerate(rels):
                v = sum(parts[r_mid.at(rel + dy - 1)][64 * dy : 64 * dy + 64] for dy in range(3))
                mskip[2 * pair + h, k] = act(v + r[:, 128 * h : 128 * h + 128]).astype(BF)
        return carry

    lax.fori_loop(0, 6, middle_conv, 0, unroll=True)

    need(s_mid, wd2, s_taps, ck, we2, s_mid_t, mmk, we1, s_fine_t, wmf, wmf9, head)

    first = lax.broadcasted_iota(jnp.int32, (64, 128), 1) < 64
    for y in range(6):
        skip = [mskip[r_skip.at(y - 2), q].astype(F32) for q in range(6)]
        turned = {q: pltpu.roll(skip[q], 64, 1) for q in (0, 5)}
        lows = [skip[2], skip[3], skip[4], skip[5], turned[0]]
        highs = [turned[5], skip[0], skip[1], skip[2], skip[3]]
        for q in range(5):
            for dx, u in enumerate(half_shifts(jnp.where(first, lows[q], highs[q]))[0]):
                at = q * 384 + dx * 128 + 64
                joined[y, at : at + 64] = u.astype(BF)
    for y in range(6):
        for z in range(10):
            v = fine[r_fine.at(y - 1), z + 9].astype(F32)
            for dx, u in enumerate((pltpu.roll(v, 1, 1), v, pltpu.roll(v, 127, 1))):
                at = 192 * z + 64 * dx + 32
                jfine[y, at : at + 32] = u.astype(BF)

    left = [
        jnp.concatenate([mskip[y, 2 * j + b] for j in range(3)], axis=1) for y in range(r_skip.count) for b in range(2)
    ]
    s = dot(jnp.concatenate(left, axis=0), s_mid[...]).astype(BF)
    for y in range(r_skip.count):
        for b in range(2):
            for c in range(2):
                at = (2 * b + c) * 64
                quarters[y, at : at + 64] = s[64 * (2 * y + b) : 64 * (2 * y + b) + 64, 256 * c : 256 * c + 256]
    cin = []
    for y in range(r_coarse.count):
        rel = 2 * (y + r_coarse.low)
        right = jnp.concatenate([quarters[r_skip.at(rel + a)] for a in range(2)], axis=0)
        cin.append(act(dot(wd2[...], right)).astype(BF))
    taps = dot(jnp.concatenate(cin, axis=0), s_taps[...]).astype(BF)
    for y in range(r_coarse.count):
        for t in range(9):
            ctaps[y, 128 * t : 128 * t + 128] = taps[128 * y : 128 * y + 128, 128 * t : 128 * t + 128]

    wc = jnp.concatenate([ck[t] for t in range(27)], axis=1)
    for first in (-1, 1):
        rels = (first, first + 1) if first < 1 else (first, first)
        cols = [jnp.concatenate([ctaps[r_coarse.at(rel + dy)] for dy in (-1, 0, 1)], axis=0) for rel in rels]
        cout = act(dot(wc, jnp.concatenate(cols, axis=1))).astype(BF)
        u = act(dot(we2[...], cout)).astype(BF)
        rows = []
        for h in range(2 if first < 1 else 1):
            for a in range(2):
                blocks = [u[(4 * a + t) * 64 : (4 * a + t) * 64 + 64, 128 * h : 128 * h + 128] for t in range(4)]
                rows.append(jnp.concatenate(blocks, axis=1))
        s = dot(jnp.concatenate(rows, axis=0), s_mid_t[...]).astype(BF)
        for i in range(len(rows)):
            for q in range(5):
                ups[2 * (first + 1) + i, q] = s[64 * i : 64 * i + 64, 128 * q : 128 * q + 128]

    for y in range(6):
        for q in range(5):
            for dx, u in enumerate(half_shifts(ups[y, q].astype(F32))[0]):
                at = q * 384 + dx * 128
                joined[y, at : at + 64] = u.astype(BF)
    wmm = jnp.concatenate(
        [
            jnp.concatenate([mmk[9 * dy + 3 * dz + dx] for dz in range(3) for dx in range(3)], axis=1)
            for dy in range(3)
        ],
        axis=0,
    )
    for k in range(3):
        parts = []
        for pair in range(3):
            cols = [joined[2 * pair + h, 384 * k : 384 * k + 1152] for h in range(2)]
            r = dot(wmm, jnp.concatenate(cols, axis=1))
            parts += [r[:, :128], r[:, 128:]]
        for y in range(4):
            v = parts[y][0:64] + parts[y + 1][64:128] + parts[y + 2][128:192]
            mout[y, k] = act(v).astype(BF)

    for y in range(4):
        for k in range(3):
            u = act(dot(we1[...], mout[y, k])).astype(BF)
            left = []
            for ab in range(4):
                left.append(jnp.concatenate([u[64 * ab : 64 * ab + 32], u[64 * ab + 32 : 64 * ab + 64]], axis=1))
            s = dot(jnp.concatenate(left, axis=0), s_fine_t[...])
            for a in range(2):
                yf = 2 * (y - 1) + a
                if not -1 <= yf <= 4:
                    continue
                for b in range(2):
                    for h in range(2):
                        zf = -2 + 2 * k + b + 6 * h
                        if not -1 <= zf <= 8:
                            continue
                        up = s[(2 * a + b) * 32 : (2 * a + b) * 32 + 32, 128 * h : 128 * h + 128]
                        for dx, u in enumerate((pltpu.roll(up, 1, 1), up, pltpu.roll(up, 127, 1))):
                            at = 192 * (zf + 1) + 64 * dx
                            jfine[yf + 1, at : at + 32] = u.astype(BF)

    for y in range(4):
        parts = []
        for pair in range(5):
            cols = []
            for h in range(2):
                at = 192 * (2 * pair + h)
                rows = [jfine[y, at : at + 192], jfine[y + 1, at : at + 192], jfine[y + 2, at : at + 128]]
                cols.append(jnp.concatenate(rows, axis=0))
            r = dot(wmf[...], jnp.concatenate(cols, axis=1))
            parts += [r[:, :128], r[:, 128:]]
        last = [jfine[y + 2, 192 * z + 128 : 192 * z + 192] for z in range(10)]
        rows = []
        for quad in range(2):
            cols = [jnp.concatenate(last[4 * quad + 2 * h : 4 * quad + 2 * h + 4], axis=0) for h in range(2)]
            r = dot(wmf9[...], jnp.concatenate(cols, axis=1))
            for i in range(4):
                z, zo, h = 4 * quad + i, i % 2, i // 2
                v = parts[z][0:32] + parts[z + 1][32:64] + parts[z + 2][64:96]
                rows.append(act(v + r[32 * zo : 32 * zo + 32, 128 * h : 128 * h + 128]).astype(BF))
        d = dot(head[...], jnp.concatenate(rows, axis=1))
        for z in range(8):
            for o in range(3):
                out[o, y, z : z + 1, :] = d[o : o + 1, 128 * z : 128 * z + 128]


def ring(axis, hops):
    count = lax.axis_size(axis)
    return [(i, (i + hops) % count) for i in range(count)]


def body(
    linear_field,
    lift_kernel,
    fine_kernel,
    reduce_first,
    middle_kernel,
    reduce_second,
    coarse_kernel,
    expand_second,
    merge_middle,
    expand_first,
    merge_fine,
    output_head,
):
    raw = [
        fine_kernel,
        reduce_first.transpose(0, 2, 1).reshape(256, 64),
        middle_kernel,
        reduce_second.transpose(0, 2, 1).reshape(512, 128),
        merge_fine,
    ]
    forms = [
        (256, 432),
        (96, 256),
        (192, 256),
        (64, 256),
        (192, 512),
        (64, 192),
        (128, 512),
        (96, 512),
        (64, 256),
        (256, 256),
        (256, 256),
        (384, 512),
        (512, 640),
        (256, 1152),
        (16, 32),
    ]
    prepared = pl.pallas_call(
        prep_kernel,
        out_shape=[jax.ShapeDtypeStruct(s, BF) for s in forms],
        in_specs=[VMEM, VMEM] + [HBM] * len(raw),
        out_specs=[HBM] * len(forms),
        scratch_shapes=[pltpu.VMEM(s, BF) for s in forms]
        + [pltpu.VMEM(w.shape, BF) for w in raw]
        + [pltpu.SemaphoreType.DMA((len(raw),)), pltpu.SemaphoreType.DMA((len(forms),))],
        cost_estimate=pl.CostEstimate(flops=4_000_000_000, bytes_accessed=10_000_000, transcendentals=0),
        compiler_params=pltpu.CompilerParams(vmem_limit_bytes=60 << 20),
    )(lift_kernel.transpose(2, 0, 1), output_head, *raw)
    count_y, count_z = lax.axis_size("gy"), lax.axis_size("gz")
    periodic = count_y == 4
    if periodic:
        own = lax.all_gather(linear_field, "gy")
        sides = []
        for hops in (1, 2):
            pairs = []
            for y in range(count_y):
                step = -hops if y % 2 == 0 else hops
                pairs += [(y * count_z + (z + step) % count_z, y * count_z + z) for z in range(count_z)]
            sides.append(lax.ppermute(own, ("gy", "gz"), pairs))
        *sides, prepared = lax.optimization_barrier((*sides, prepared))
        swap = [(y, y + 1 - 2 * (y % 2)) for y in range(count_y)]
        fields = [own, *sides, *(lax.ppermute(side, "gy", swap) for side in sides)]
    else:
        send = functools.partial(lax.ppermute, axis_name="gz")
        below = send(linear_field, perm=ring("gz", 1))
        above = send(linear_field, perm=ring("gz", -1))
        below_2 = send(linear_field[:, :, 4:], perm=ring("gz", 2))
        above_2 = send(linear_field[:, :, :4], perm=ring("gz", -2))
        wide = jnp.concatenate([below_2, below, linear_field, above, above_2], axis=2)
        fields = [
            jnp.stack([wide if h == 0 else lax.ppermute(wide, "gy", ring("gy", -h)) for h in range(-3, 4)])
        ]

    t_w, wf, wf9, wd1, wm, wm9, wd2, wmf, wmf9, split_f, split_ft, split_m, split_mt, taps, head = prepared

    r_lin, r_lift, r_fine, r_mid, r_skip, r_coarse = levels(periodic)
    scratch = [
        pltpu.VMEM((r_lin.count, 4, 144, 128), BF),
        pltpu.VMEM((r_lift.count, 30 * 96, 128), BF),
        pltpu.VMEM((r_fine.count, 28, 32, 128), BF),
        pltpu.VMEM((r_fine.count, 7, 128, 128), BF),
        pltpu.VMEM((r_skip.count, 6, 64, 128), BF),
        pltpu.VMEM((r_skip.count, 256, 256), BF),
        pltpu.VMEM((r_coarse.count, 1152, 128), BF),
        pltpu.VMEM((6, 5, 64, 128), BF),
        pltpu.VMEM((4, 3, 64, 128), BF),
        pltpu.VMEM((6, 5 * 384, 128), BF),
        pltpu.VMEM((6, 10 * 192, 128), BF),
    ]
    weights = [
        t_w,
        wf,
        wf9,
        split_f,
        wd1,
        wm,
        wm9,
        split_m,
        wd2,
        taps,
        coarse_kernel,
        expand_second.reshape(512, 128),
        split_mt,
        merge_middle,
        expand_first.reshape(256, 64),
        split_ft,
        wmf,
        wmf9,
        head,
    ]
    scratch += [pltpu.VMEM(w.shape, BF) for w in weights]
    scratch.append(pltpu.SemaphoreType.DMA((len(weights),)))
    scratch += [pltpu.VMEM(f.shape, BF) for f in fields] + [pltpu.SemaphoreType.DMA((len(fields),))]
    return pl.pallas_call(
        functools.partial(net_kernel, periodic),
        out_shape=jax.ShapeDtypeStruct(linear_field.shape, F32),
        in_specs=[ANY] * len(fields) + [HBM] * len(weights),
        out_specs=VMEM,
        scratch_shapes=scratch,
        compiler_params=pltpu.CompilerParams(vmem_limit_bytes=60 << 20),
    )(*fields, *weights)


def solution(mesh):
    return jax.shard_map(
        body,
        mesh=mesh,
        in_specs=(P(None, "gy", "gz", None), P(), P(), P(), P(), P(), P(), P(), P(), P(), P(), P()),
        out_specs=P(None, "gy", "gz", None),
        check_vma=False,
    )
```

```python
import functools

import jax
import jax.numpy as jnp
from jax import lax
from jax.experimental import pallas as pl
from jax.experimental.pallas import tpu as pltpu
from jax.sharding import PartitionSpec as P

BF = jnp.bfloat16
F32 = jnp.float32
VMEM = pl.BlockSpec(memory_space=pltpu.VMEM)
ANY = pl.BlockSpec(memory_space=pl.ANY)
HBM = pl.BlockSpec(memory_space=pltpu.HBM)
SMEM = pl.BlockSpec(memory_space=pltpu.SMEM)


def act(values):
    return jnp.maximum(values, 0.1 * values)


def dot(left, right):
    return jnp.dot(left, right, preferred_element_type=F32)


def iotas(rows, columns):
    return (
        lax.broadcasted_iota(jnp.int32, (rows, columns), 0),
        lax.broadcasted_iota(jnp.int32, (rows, columns), 1),
    )


def chosen(test):
    return jnp.where(test, 1.0, 0.0).astype(BF)


def fine_order(i):
    return ((i & 1) << 7) | ((i >> 7) << 6) | ((i & 127) >> 1)


def split_middle():
    r, c = iotas(384, 512)
    return chosen((((r & 1) << 8) | (((r >> 7) + 3 * ((r >> 6) & 1)) << 5) | ((r & 63) >> 1)) == c)


def join_middle():
    r, c = iotas(512, 640)
    source = ((2 * ((r >> 5) & 3) + (r >> 8)) << 6) | ((r & 31) << 1) | ((r >> 7) & 1)
    return chosen(source == ((((c >> 7) + 3 * ((c >> 6) & 1)) << 6) | (c & 63)))


def coarse_tap(dz, dx):
    r, c = iotas(256, 128)
    return chosen(r == ((((c >> 5) + dz) << 5) | ((c + dx - 1) & 31)))


def lift_spread(c):
    r, col = iotas(27, 512)
    return chosen(col == ((r // 9 * 3 + c) * 3 + r % 3) * 16 + r // 3 % 3)


def prep_kernel(lift, head, *refs):
    sources, refs = refs[:5], refs[5:]
    results, refs = refs[:15], refs[15:]
    (t_o, wf_o, wf9_o, wd1_o, wm_o, wm9_o, wd2_o, wmf_o, wmf9_o, sf_o, sft_o, sm_o, smt_o, st_o, head_o), refs = refs[:15], refs[15:]
    (fine, red1, mid, red2, mfine), sems, out_sems = refs[:5], refs[5], refs[6]
    copies = [pltpu.make_async_copy(src, dst, sems.at[i]) for i, (src, dst) in enumerate(zip(sources, refs))]
    for copy in copies:
        copy.start()
    r, c = iotas(256, 256)
    sf_o[...] = chosen(fine_order(r) == c)
    sft_o[...] = chosen(r == fine_order(c))
    head_o[...] = jnp.concatenate([head[...].astype(F32), jnp.zeros((13, 32), F32)], axis=0).astype(BF)
    sm_o[...] = split_middle()
    smt_o[...] = join_middle()
    for t in range(9):
        st_o[:, 128 * t : 128 * t + 128] = coarse_tap(t // 3, t % 3)
    base = sum(
        lax.dot_general(lift[c], lift_spread(c), (((0,), (0,)), ((), ())), preferred_element_type=F32)
        for c in range(3)
    )
    for zo in range(8):
        moved = base if zo == 0 else pltpu.roll(base, zo, 1)
        t_o[32 * zo : 32 * zo + 32] = moved[:, :432].astype(BF)
    for copy in copies:
        copy.wait()
    wf9_o[...] = jnp.zeros_like(wf9_o)
    wmf9_o[...] = jnp.zeros_like(wmf9_o)
    for dz in range(3):
        for dy in range(3):
            for dx in range(3):
                k = 3 * dy + dx
                if k < 8:
                    wf_o[32 * dz : 32 * dz + 32, 32 * k : 32 * k + 32] = fine[9 * dy + 3 * dz + dx]
                else:
                    for zo in range(6):
                        wf9_o[32 * zo : 32 * zo + 32, 32 * (dz + zo) : 32 * (dz + zo) + 32] = fine[9 * dy + 3 * dz + dx]
                if k < 8:
                    wmf_o[32 * dz : 32 * dz + 32, 64 * k : 64 * k + 64] = mfine[9 * dy + 3 * dz + dx]
                else:
                    for zo in range(2):
                        at = 64 * (dz + zo)
                        wmf9_o[32 * zo : 32 * zo + 32, at : at + 64] = mfine[9 * dy + 3 * dz + dx]
                j = 3 * dz + dx
                if j < 8:
                    wm_o[64 * dy : 64 * dy + 64, 64 * j : 64 * j + 64] = mid[9 * dy + 3 * dz + dx]
                else:
                    wm9_o[:, 64 * dy : 64 * dy + 64] = mid[9 * dy + 3 * dz + dx]
    wd1_o[...] = red1[...].astype(F32).T.astype(BF)
    wd2_o[...] = red2[...].astype(F32).T.astype(BF)
    made = (t_o, wf_o, wf9_o, wd1_o, wm_o, wm9_o, wd2_o, wmf_o, wmf9_o, sf_o, sft_o, sm_o, smt_o, st_o, head_o)
    copies = [pltpu.make_async_copy(src, dst, out_sems.at[i]) for i, (src, dst) in enumerate(zip(made, results))]
    for copy in copies:
        copy.start()
    for copy in copies:
        copy.wait()


class Rows:
    def __init__(self, low, count, periodic):
        self.low, self.count, self.periodic = low, count, periodic

    def at(self, rel):
        if self.periodic:
            moved = rel - self.low + 4 * self.count
            return moved % self.count if isinstance(moved, int) else lax.rem(moved, self.count)
        return rel - self.low


def levels(periodic):
    if periodic:
        fine, mid, coarse = Rows(-8, 16, True), Rows(-4, 8, True), Rows(-2, 4, True)
        return fine, fine, fine, mid, mid, coarse
    return (
        Rows(-12, 28, False),
        Rows(-11, 26, False),
        Rows(-10, 24, False),
        Rows(-5, 12, False),
        Rows(-4, 10, False),
        Rows(-2, 5, False),
    )


def half_shifts(v):
    lane = lax.broadcasted_iota(jnp.int32, v.shape, 1) & 63
    t = pltpu.roll(v, 64, 1)
    low_v, low_t, high_v, high_t = (pltpu.roll(u, n, 1) for n in (1, 127) for u in (v, t))
    low, high = lane == 0, lane == 63
    return (
        (jnp.where(low, low_t, low_v), v, jnp.where(high, high_t, high_v)),
        (jnp.where(low, low_v, low_t), t, jnp.where(high, high_v, high_t)),
    )


def net_kernel(periodic, *refs):
    count = 5 if periodic else 1
    fields, refs = refs[:count], refs[count:]
    weights, out, refs = refs[:19], refs[19], refs[20:]
    pat, lifted, fine, halves, mskip, quarters, ctaps, ups, mout, joined, jfine, mids = refs[:12]
    held, sems = refs[12:31], refs[31]
    near_by, field_sems = refs[32 : 32 + count], refs[32 + count]
    field_copies = [
        pltpu.make_async_copy(src, dst, field_sems.at[i]) for i, (src, dst) in enumerate(zip(fields, near_by))
    ]
    for copy in field_copies:
        copy.start()
    copies = [pltpu.make_async_copy(src, dst, sems.at[i]) for i, (src, dst) in enumerate(zip(weights, held))]
    copies[0].start()
    if periodic:
        own, near, far, other_near, other_far = near_by
    else:
        wide = near_by[0]
    (t_w, wf, wf9, s_fine, wd1, wm, wm9, s_mid, wd2, s_taps, ck, we2, s_mid_t, mmk, we1, s_fine_t, wmf, wmf9, head) = held

    def need(*names):
        for name in names:
            copies[[h is name for h in held].index(True)].wait()

    r_lin, r_lift, r_fine, r_mid, r_skip, r_coarse = levels(periodic)
    me = lax.axis_index("gy")
    core = lax.rem(me, 2)

    for copy in field_copies:
        copy.wait()

    def patch(k, carry):
        for c in range(3):
            if periodic:
                block = lax.rem(me + k + 2, 4)
                mine, by, away, other_by, other_away = (
                    ref[block, c].astype(F32) for ref in (own, near, far, other_near, other_far)
                )
                below = jnp.where(core == 0, by, other_by), jnp.where(core == 0, away, other_away)
                above = jnp.where(core == 0, other_by, by), jnp.where(core == 0, other_away, away)
            for row in range(4):
                if periodic:
                    at = slice(8 * row, 8 * row + 8)
                    parts = [below[1][at][4:], below[0][at], mine[at], above[0][at], above[1][at][:4]]
                    v = jnp.concatenate([*parts, jnp.zeros((8, 128), F32)], axis=0)
                else:
                    v = jnp.concatenate([wide[k, c, row].astype(F32), jnp.zeros((8, 128), F32)], axis=0)
                for dx, u in enumerate((pltpu.roll(v, 1, 1), v, pltpu.roll(v, 127, 1))):
                    for j in range(4):
                        at_k = (3 * c + dx) * 16
                        pat[4 * k + row, j, at_k : at_k + 16] = u[8 * j : 8 * j + 16].astype(BF)
        return carry

    lax.fori_loop(0, r_lin.count // 4, patch, 0, unroll=2 if periodic else 1)
    for copy in copies[1:]:
        copy.start()

    need(t_w)

    def lift(k, carry):
        rel = k + r_lift.low
        ys = [r_lin.at(rel + dy) for dy in (-1, 0, 1)]
        for pair in range(2):
            cols = [jnp.concatenate([pat[y, 2 * pair + h] for y in ys], axis=0) for h in range(2)]
            r = act(dot(t_w[...], jnp.concatenate(cols, axis=1)))
            for h in range(2):
                for zo in range(8):
                    z = 16 * pair + 8 * h + zo
                    if z < 30:
                        v = r[32 * zo : 32 * zo + 32, 128 * h : 128 * h + 128]
                        lifted[k, 96 * z : 96 * z + 32] = pltpu.roll(v, 1, 1).astype(BF)
                        lifted[k, 96 * z + 32 : 96 * z + 64] = v.astype(BF)
                        lifted[k, 96 * z + 64 : 96 * z + 96] = pltpu.roll(v, 127, 1).astype(BF)
        return carry

    lax.fori_loop(0, r_lift.count, lift, 0, unroll=8)

    need(wf, wf9, s_fine, wd1)

    def fine_conv(k, carry):
        rel = k + r_fine.low
        ys = [r_lift.at(rel + dy) for dy in (-1, 0, 1)]
        parts = []
        for pair in range(15):
            cols = [
                jnp.concatenate([*(lifted[y, 96 * (2 * pair + h) : 96 * (2 * pair + h) + 96] for y in ys[:2]), lifted[ys[2], 96 * (2 * pair + h) : 96 * (2 * pair + h) + 64]], axis=0)
                for h in range(2)
            ]
            r = dot(wf[...], jnp.concatenate(cols, axis=1))
            parts += [r[:, :128], r[:, 128:]]
        rows = []
        last = [lifted[ys[2], 96 * z + 64 : 96 * z + 96] for z in range(30)]
        for first, outs in ((0, 6), (12, 6), (24, 2)):
            cols = [jnp.concatenate(last[first + outs * h : first + outs * h + outs + 2], axis=0) for h in range(2)]
            r = dot(wf9[: 32 * outs, : 32 * outs + 64], jnp.concatenate(cols, axis=1))
            for i in range(2 * outs):
                z, zo, h = first + i, i % outs, i // outs
                v = parts[z][0:32] + parts[z + 1][32:64] + parts[z + 2][64:96]
                v = act(v + r[32 * zo : 32 * zo + 32, 128 * h : 128 * h + 128]).astype(BF)
                fine[k, z] = v
                rows.append(v)
        left = [jnp.concatenate([rows[z], rows[z + 14]], axis=1) for z in range(14)]
        s = dot(jnp.concatenate(left, axis=0), s_fine[...]).astype(BF)
        for i in range(14):
            for c in range(2):
                halves[k, i // 2, (2 * (i % 2) + c) * 32 : (2 * (i % 2) + c) * 32 + 32] = s[
                    32 * i : 32 * i + 32, 128 * c : 128 * c + 128
                ]
        return carry

    def middle_in(k, carry):
        direct = [[], []]
        for p in range(7):
            cols = []
            for h in range(2):
                rel = 2 * (2 * k + h + r_mid.low)
                cols.append(jnp.concatenate([halves[r_fine.at(rel + a), p] for a in range(2)], axis=0))
            r = act(dot(wd1[...], jnp.concatenate(cols, axis=1)))
            for h in range(2):
                direct[h].append(r[:, 128 * h : 128 * h + 128])
        first = lax.broadcasted_iota(jnp.int32, (64, 128), 1) < 64
        for h in range(2):
            kept, turned = zip(*(half_shifts(v.astype(BF)) for v in direct[h]))
            lows = [*kept, turned[0]]
            highs = [turned[6], *kept]
            for q in range(8):
                for dx in range(3):
                    at = q * 192 + dx * 64
                    mids[2 * k + h, at : at + 64] = jnp.where(first, lows[q][dx], highs[q][dx])
        return carry

    def down(k, carry):
        for j in range(4):
            fine_conv(4 * k + j, carry)
        return middle_in(k, carry)

    lax.fori_loop(0, r_mid.count // 2, down, 0, unroll=4 if periodic else 1)

    need(wm, wm9)

    def middle_conv(k, carry):
        parts = []
        start = pl.multiple_of(k * 192, 192)
        for pair in range(r_mid.count // 2):
            cols = [mids[2 * pair + h, pl.ds(start, 512)] for h in range(2)]
            r = dot(wm[...], jnp.concatenate(cols, axis=1))
            parts += [r[:, :128], r[:, 128:]]
        last = [mids[y, pl.ds(start + 512, 64)] for y in range(r_mid.count)]
        for pair in range(r_skip.count // 2):
            rels = [2 * pair + h + r_skip.low for h in range(2)]
            cols = [jnp.concatenate([last[r_mid.at(rel + dy)] for dy in (-1, 0, 1)], axis=0) for rel in rels]
            r = dot(wm9[...], jnp.concatenate(cols, axis=1))
            for h, rel in enumerate(rels):
                v = sum(parts[r_mid.at(rel + dy - 1)][64 * dy : 64 * dy + 64] for dy in range(3))
                mskip[2 * pair + h, k] = act(v + r[:, 128 * h : 128 * h + 128]).astype(BF)
        return carry

    lax.fori_loop(0, 6, middle_conv, 0, unroll=True)

    need(s_mid, wd2, s_taps, ck, we2, s_mid_t, mmk, we1, s_fine_t, wmf, wmf9, head)

    first = lax.broadcasted_iota(jnp.int32, (64, 128), 1) < 64
    for y in range(6):
        skip = [mskip[r_skip.at(y - 2), q].astype(F32) for q in range(6)]
        turned = {q: pltpu.roll(skip[q], 64, 1) for q in (0, 5)}
        lows = [skip[2], skip[3], skip[4], skip[5], turned[0]]
        highs = [turned[5], skip[0], skip[1], skip[2], skip[3]]
        for q in range(5):
            for dx, u in enumerate(half_shifts(jnp.where(first, lows[q], highs[q]))[0]):
                at = q * 384 + dx * 128 + 64
                joined[y, at : at + 64] = u.astype(BF)
    for y in range(6):
        for z in range(10):
            v = fine[r_fine.at(y - 1), z + 9].astype(F32)
            for dx, u in enumerate((pltpu.roll(v, 1, 1), v, pltpu.roll(v, 127, 1))):
                at = 192 * z + 64 * dx + 32
                jfine[y, at : at + 32] = u.astype(BF)

    left = [
        jnp.concatenate([mskip[y, 2 * j + b] for j in range(3)], axis=1) for y in range(r_skip.count) for b in range(2)
    ]
    s = dot(jnp.concatenate(left, axis=0), s_mid[...]).astype(BF)
    for y in range(r_skip.count):
        for b in range(2):
            for c in range(2):
                at = (2 * b + c) * 64
                quarters[y, at : at + 64] = s[64 * (2 * y + b) : 64 * (2 * y + b) + 64, 256 * c : 256 * c + 256]
    cin = []
    for y in range(r_coarse.count):
        rel = 2 * (y + r_coarse.low)
        right = jnp.concatenate([quarters[r_skip.at(rel + a)] for a in range(2)], axis=0)
        cin.append(act(dot(wd2[...], right)).astype(BF))
    taps = dot(jnp.concatenate(cin, axis=0), s_taps[...]).astype(BF)
    for y in range(r_coarse.count):
        for t in range(9):
            ctaps[y, 128 * t : 128 * t + 128] = taps[128 * y : 128 * y + 128, 128 * t : 128 * t + 128]

    wc = jnp.concatenate([ck[t] for t in range(27)], axis=1)
    for first in (-1, 1):
        rels = (first, first + 1) if first < 1 else (first, first)
        cols = [jnp.concatenate([ctaps[r_coarse.at(rel + dy)] for dy in (-1, 0, 1)], axis=0) for rel in rels]
        cout = act(dot(wc, jnp.concatenate(cols, axis=1))).astype(BF)
        u = act(dot(we2[...], cout)).astype(BF)
        rows = []
        for h in range(2 if first < 1 else 1):
            for a in range(2):
                blocks = [u[(4 * a + t) * 64 : (4 * a + t) * 64 + 64, 128 * h : 128 * h + 128] for t in range(4)]
                rows.append(jnp.concatenate(blocks, axis=1))
        s = dot(jnp.concatenate(rows, axis=0), s_mid_t[...]).astype(BF)
        for i in range(len(rows)):
            for q in range(5):
                ups[2 * (first + 1) + i, q] = s[64 * i : 64 * i + 64, 128 * q : 128 * q + 128]

    for y in range(6):
        for q in range(5):
            for dx, u in enumerate(half_shifts(ups[y, q].astype(F32))[0]):
                at = q * 384 + dx * 128
                joined[y, at : at + 64] = u.astype(BF)
    wmm = jnp.concatenate(
        [
            jnp.concatenate([mmk[9 * dy + 3 * dz + dx] for dz in range(3) for dx in range(3)], axis=1)
            for dy in range(3)
        ],
        axis=0,
    )
    for k in range(3):
        parts = []
        for pair in range(3):
            cols = [joined[2 * pair + h, 384 * k : 384 * k + 1152] for h in range(2)]
            r = dot(wmm, jnp.concatenate(cols, axis=1))
            parts += [r[:, :128], r[:, 128:]]
        for y in range(4):
            v = parts[y][0:64] + parts[y + 1][64:128] + parts[y + 2][128:192]
            mout[y, k] = act(v).astype(BF)

    for y in range(4):
        for k in range(3):
            u = act(dot(we1[...], mout[y, k])).astype(BF)
            left = []
            for ab in range(4):
                left.append(jnp.concatenate([u[64 * ab : 64 * ab + 32], u[64 * ab + 32 : 64 * ab + 64]], axis=1))
            s = dot(jnp.concatenate(left, axis=0), s_fine_t[...])
            for a in range(2):
                yf = 2 * (y - 1) + a
                if not -1 <= yf <= 4:
                    continue
                for b in range(2):
                    for h in range(2):
                        zf = -2 + 2 * k + b + 6 * h
                        if not -1 <= zf <= 8:
                            continue
                        up = s[(2 * a + b) * 32 : (2 * a + b) * 32 + 32, 128 * h : 128 * h + 128]
                        for dx, u in enumerate((pltpu.roll(up, 1, 1), up, pltpu.roll(up, 127, 1))):
                            at = 192 * (zf + 1) + 64 * dx
                            jfine[yf + 1, at : at + 32] = u.astype(BF)

    for y in range(4):
        parts = []
        for pair in range(5):
            cols = []
            for h in range(2):
                at = 192 * (2 * pair + h)
                rows = [jfine[y, at : at + 192], jfine[y + 1, at : at + 192], jfine[y + 2, at : at + 128]]
                cols.append(jnp.concatenate(rows, axis=0))
            r = dot(wmf[...], jnp.concatenate(cols, axis=1))
            parts += [r[:, :128], r[:, 128:]]
        last = [jfine[y + 2, 192 * z + 128 : 192 * z + 192] for z in range(10)]
        rows = []
        for quad in range(2):
            cols = [jnp.concatenate(last[4 * quad + 2 * h : 4 * quad + 2 * h + 4], axis=0) for h in range(2)]
            r = dot(wmf9[...], jnp.concatenate(cols, axis=1))
            for i in range(4):
                z, zo, h = 4 * quad + i, i % 2, i // 2
                v = parts[z][0:32] + parts[z + 1][32:64] + parts[z + 2][64:96]
                rows.append(act(v + r[32 * zo : 32 * zo + 32, 128 * h : 128 * h + 128]).astype(BF))
        d = dot(head[...], jnp.concatenate(rows, axis=1))
        for z in range(8):
            for o in range(3):
                out[o, y, z : z + 1, :] = d[o : o + 1, 128 * z : 128 * z + 128]


def ring(axis, hops):
    count = lax.axis_size(axis)
    return [(i, (i + hops) % count) for i in range(count)]


def body(
    linear_field,
    lift_kernel,
    fine_kernel,
    reduce_first,
    middle_kernel,
    reduce_second,
    coarse_kernel,
    expand_second,
    merge_middle,
    expand_first,
    merge_fine,
    output_head,
):
    raw = [
        fine_kernel,
        reduce_first.transpose(0, 2, 1).reshape(256, 64),
        middle_kernel,
        reduce_second.transpose(0, 2, 1).reshape(512, 128),
        merge_fine,
    ]
    forms = [
        (256, 432),
        (96, 256),
        (192, 256),
        (64, 256),
        (192, 512),
        (64, 192),
        (128, 512),
        (96, 512),
        (64, 256),
        (256, 256),
        (256, 256),
        (384, 512),
        (512, 640),
        (256, 1152),
        (16, 32),
    ]
    prepared = pl.pallas_call(
        prep_kernel,
        out_shape=[jax.ShapeDtypeStruct(s, BF) for s in forms],
        in_specs=[VMEM, VMEM] + [HBM] * len(raw),
        out_specs=[HBM] * len(forms),
        scratch_shapes=[pltpu.VMEM(s, BF) for s in forms]
        + [pltpu.VMEM(w.shape, BF) for w in raw]
        + [pltpu.SemaphoreType.DMA((len(raw),)), pltpu.SemaphoreType.DMA((len(forms),))],
        cost_estimate=pl.CostEstimate(flops=4_000_000_000, bytes_accessed=10_000_000, transcendentals=0),
        compiler_params=pltpu.CompilerParams(vmem_limit_bytes=60 << 20),
    )(lift_kernel.transpose(2, 0, 1), output_head, *raw)
    count_y, count_z = lax.axis_size("gy"), lax.axis_size("gz")
    periodic = count_y == 4
    if periodic:
        own = lax.all_gather(linear_field.reshape(3, 32, 128), "gy")
        sides = []
        for hops in (1, 2):
            pairs = []
            for y in range(count_y):
                step = -hops if y % 2 == 0 else hops
                pairs += [(y * count_z + (z + step) % count_z, y * count_z + z) for z in range(count_z)]
            sides.append(lax.ppermute(own, ("gy", "gz"), pairs))
        *sides, prepared = lax.optimization_barrier((*sides, prepared))
        swap = [(y, y + 1 - 2 * (y % 2)) for y in range(count_y)]
        fields = [own, *sides, *(lax.ppermute(side, "gy", swap) for side in sides)]
    else:
        send = functools.partial(lax.ppermute, axis_name="gz")
        below = send(linear_field, perm=ring("gz", 1))
        above = send(linear_field, perm=ring("gz", -1))
        below_2 = send(linear_field[:, :, 4:], perm=ring("gz", 2))
        above_2 = send(linear_field[:, :, :4], perm=ring("gz", -2))
        wide = jnp.concatenate([below_2, below, linear_field, above, above_2], axis=2)
        fields = [
            jnp.stack([wide if h == 0 else lax.ppermute(wide, "gy", ring("gy", -h)) for h in range(-3, 4)])
        ]

    t_w, wf, wf9, wd1, wm, wm9, wd2, wmf, wmf9, split_f, split_ft, split_m, split_mt, taps, head = prepared

    r_lin, r_lift, r_fine, r_mid, r_skip, r_coarse = levels(periodic)
    scratch = [
        pltpu.VMEM((r_lin.count, 4, 144, 128), BF),
        pltpu.VMEM((r_lift.count, 30 * 96, 128), BF),
        pltpu.VMEM((r_fine.count, 28, 32, 128), BF),
        pltpu.VMEM((r_fine.count, 7, 128, 128), BF),
        pltpu.VMEM((r_skip.count, 6, 64, 128), BF),
        pltpu.VMEM((r_skip.count, 256, 256), BF),
        pltpu.VMEM((r_coarse.count, 1152, 128), BF),
        pltpu.VMEM((6, 5, 64, 128), BF),
        pltpu.VMEM((4, 3, 64, 128), BF),
        pltpu.VMEM((6, 5 * 384, 128), BF),
        pltpu.VMEM((6, 10 * 192, 128), BF),
        pltpu.VMEM((r_mid.count, 8 * 192, 128), BF),
    ]
    weights = [
        t_w,
        wf,
        wf9,
        split_f,
        wd1,
        wm,
        wm9,
        split_m,
        wd2,
        taps,
        coarse_kernel,
        expand_second.reshape(512, 128),
        split_mt,
        merge_middle,
        expand_first.reshape(256, 64),
        split_ft,
        wmf,
        wmf9,
        head,
    ]
    scratch += [pltpu.VMEM(w.shape, BF) for w in weights]
    scratch.append(pltpu.SemaphoreType.DMA((len(weights),)))
    scratch += [pltpu.VMEM(f.shape, BF) for f in fields] + [pltpu.SemaphoreType.DMA((len(fields),))]
    return pl.pallas_call(
        functools.partial(net_kernel, periodic),
        out_shape=jax.ShapeDtypeStruct(linear_field.shape, F32),
        in_specs=[ANY] * len(fields) + [HBM] * len(weights),
        out_specs=VMEM,
        scratch_shapes=scratch,
        compiler_params=pltpu.CompilerParams(vmem_limit_bytes=60 << 20),
    )(*fields, *weights)


def solution(mesh):
    return jax.shard_map(
        body,
        mesh=mesh,
        in_specs=(P(None, "gy", "gz", None), P(), P(), P(), P(), P(), P(), P(), P(), P(), P(), P()),
        out_specs=P(None, "gy", "gz", None),
        check_vma=False,
    )
```
